512 devices in a mesh: rep: 16 (over z_lo, x), fsdp: 32 (over z_hi, y, core).
Axes of the slice: x: 4, y: 4, z: 16 (z_hi: 4, z_lo: 4; z = z_hi * 4 + z_lo), core: 2. Of those that a mesh axis runs over, the one named last changes fastest.
Arguments:
- residual_in: bfloat16 [16, 12288, 2048], P('rep', 'fsdp'), may hold values from -6 to 6
- norm_gain: float32 [16, 2048], P('rep'), may hold values from 0.5 to 1.5
- kv_weight: bfloat16 [16, 2048, 1024], P('rep', 'fsdp'), may hold values from -0.125 to 0.125
- kv_grad: bfloat16 [16, 12288, 1024], P('rep', 'fsdp'), may hold values from -6 to 6
- outer_delta: float32 [16, 512, 2048], P('rep', 'fsdp'), may hold values from -6 to 6
- outer_momentum: float32 [512, 2048], P('fsdp'), may hold values from -6 to 6
- global_params: float32 [512, 2048], P('fsdp'), may hold values from -6 to 6
- sync_index: int32 [1], replicated, may hold values from 0 to 63
Outputs:
- grad_kv: bfloat16 [16, 2048, 1024], P('rep', 'fsdp')
- grad_gain: float32 [16, 2048], P('rep')
- grad_input: bfloat16 [16, 12288, 2048], P('rep', 'fsdp')
- new_params: float32 [512, 2048], P('fsdp')
- new_momentum: float32 [512, 2048], P('fsdp')
The draws below stay inside these ranges and needn't reach their ends.
All inputs are finite; a program needn't handle non-finite values.
Results may differ from the reference program's by a relative error of at most 0.023.
Values may be sent and summed in bfloat16 or wider, within the bound.
A program may use at most 64 MiB of HBM per device.

```python
import jax
import jax.numpy as jnp
from jax import lax

D = 2048
TOK_DEV = 384
ROUNDS = 64
KVW = 1024
TOKENS = 12288
FRAG = 512
REPS = 16
N_REP = 16
N_FSDP = 32


def block_scale(rng, extent, shards, smallest, largest):
    def one(dim, blocks):
        heights = jax.random.uniform(jax.random.fold_in(jax.random.fold_in(rng, 6), dim), (blocks,), jnp.float32, smallest / len(shards), largest / len(shards))
        return jnp.repeat(jnp.exp(heights), extent[dim] // blocks).reshape((-1,) + (1,) * (len(extent) - dim - 1))

    loudness = one(*shards[0])
    for cut in shards[1:]:
        loudness = loudness * one(*cut)
    return loudness


def gaussian(rng, extent, deviation, most, cuts=(), kind=jnp.bfloat16):
    level = block_scale(rng, extent, cuts, -0.22, 0.18) if cuts else 1.0
    array = jax.random.normal(rng, extent, jnp.float32) * deviation * level
    return jnp.minimum(jnp.maximum(array, -most), most).astype(kind)


def setup_inputs(seed: int = 0) -> dict:
    key_of = jax.random.split(jax.random.key(seed), 9)
    return {
        "residual_in": gaussian(key_of[0], (REPS, TOKENS, D), 1.0, 6.0, ((0, 16), (1, 32))),
        "norm_gain": jnp.clip(1.0 + 0.1 * jax.random.normal(key_of[1], (REPS, D), jnp.float32), 0.5, 1.5),
        "kv_weight": gaussian(key_of[2], (REPS, D, KVW), D ** -0.5, 0.125, ((0, 16), (1, 32))),
        "kv_grad": gaussian(key_of[3], (REPS, TOKENS, KVW), 1.0, 6.0, ((0, 16), (1, 32))),
        "outer_delta": gaussian(key_of[4], (REPS, FRAG, D), 1.0, 6.0, ((0, 16), (1, 32)), jnp.float32),
        "outer_momentum": gaussian(key_of[5], (FRAG, D), 1.0, 6.0, ((0, 32),), jnp.float32),
        "global_params": gaussian(key_of[6], (FRAG, D), 1.0, 6.0, ((0, 32),), jnp.float32),
        "sync_index": jax.random.randint(key_of[7], (1,), 0, ROUNDS).astype(jnp.int32),
    }


EPSILON = 1e-05
NESTEROV_MU = 0.9
OUTER_RATE = 0.7

def replica_step(inputs):
    residual_in, norm_gain, kv_weight, kv_grad = inputs
    resid = residual_in.astype(jnp.float32)
    scale = lax.rsqrt(lax.optimization_barrier(jnp.mean(resid * resid, axis=-1, keepdims=True)) + EPSILON)
    unit = resid * scale
    normed = (unit * norm_gain).astype(jnp.bfloat16)
    normed_blocks = normed.reshape(N_FSDP, TOK_DEV, D)
    grad_blocks = kv_grad.reshape(N_FSDP, TOK_DEV, KVW)

    def add_block(total, pieces):
        left, right = pieces
        term = jnp.dot(left.T, right, preferred_element_type=jnp.float32)
        rounded = lax.optimization_barrier(term.astype(jnp.bfloat16))
        return (total + rounded.astype(jnp.float32), None)
    weight_total, unused = lax.scan(add_block, jnp.zeros((D, KVW), jnp.float32), (normed_blocks, grad_blocks))
    grad_kv = weight_total.astype(jnp.bfloat16)
    normed_grad = jnp.dot(kv_grad, kv_weight.T, preferred_element_type=jnp.float32)
    grad_gain = lax.optimization_barrier(jnp.sum(normed_grad * unit, axis=0))
    scaled = norm_gain * normed_grad
    inner = lax.optimization_barrier(jnp.mean(scaled * unit, axis=-1, keepdims=True))
    grad_input = (scale * (scaled - unit * inner)).astype(jnp.bfloat16)
    return (grad_kv, grad_gain, grad_input)

def reference(residual_in, norm_gain, kv_weight, kv_grad, outer_delta, outer_momentum, global_params, sync_index):
    grad_kv, grad_gain, grad_input = lax.map(replica_step, (residual_in, norm_gain, kv_weight, kv_grad))
    mean_delta = lax.optimization_barrier(jnp.sum(outer_delta, axis=0)) / N_REP
    phase = sync_index[0].astype(jnp.float32) / ROUNDS
    rate = OUTER_RATE * (1.0 + jnp.cos(jnp.pi * phase)) / 2.0
    new_momentum = NESTEROV_MU * outer_momentum + mean_delta
    new_params = global_params - rate * (mean_delta + NESTEROV_MU * new_momentum)
    return (grad_kv, grad_gain, grad_input, new_params, new_momentum)
```

```python
import functools

import jax
import jax.numpy as jnp
from jax import lax
from jax.experimental import pallas as pl
from jax.experimental.pallas import tpu as pltpu
from jax.sharding import PartitionSpec as P

ROUNDS = 64
EPSILON = 1e-05
NESTEROV_MU = 0.9
OUTER_RATE = 0.7
MESH = pl.DeviceIdType.MESH
F32, BF16 = jnp.float32, jnp.bfloat16
LANES = 128


def kernel(
    sizes,
    resid_hbm,
    gain_hbm,
    w_hbm,
    kv_hbm,
    delta_hbm,
    mom_hbm,
    par_hbm,
    sync_ref,
    gkv_out,
    ggain_out,
    gin_hbm,
    npar_out,
    nmom_out,
    x,
    gain,
    wbuf,
    kv,
    kv_sib,
    nt,
    nt_sib,
    pb,
    ybuf,
    yb,
    zbuf,
    scale,
    acc,
    gb,
    obuf,
    gs,
    gsib,
    gy,
    gz,
    delta,
    mom,
    par,
    dl,
    dx,
    dz,
    dt,
    sem_in,
    sem_out,
    az_s,
    az_r,
    ay_s,
    ay_r,
    as_s,
    as_r,
    nt_s,
    nt_r,
    ry_s,
    ry_r,
    rz_s,
    rz_r,
    ox_s,
    ox_r,
    og_s,
    og_r,
    gg_s,
    gg_r,
):
    tok, feat, kvw, outer = sizes
    rows = w_hbm.shape[0]
    half = rows // 2
    pair = 2 * rows
    chunks = feat // pair
    f = lax.axis_index("fsdp")
    c = lax.rem(f, 2)
    y = lax.rem(lax.div(f, 2), 4)
    h = lax.div(f, 8)
    rep = lax.axis_index("rep")
    xx = lax.rem(rep, 4)
    zl = lax.div(rep, 4)

    def mod4(v):
        return lax.rem(v + 8, 4)

    def inside(hh, yy, cc):
        return {"fsdp": (hh * 4 + yy) * 2 + cc}

    sib = inside(h, y, 1 - c)
    y_peer = {s: inside(h, mod4(y + s), c) for s in (1, -1, 2)}
    h_peer = {s: inside(mod4(h + s), y, c) for s in (1, -1, 2)}
    x_peer = {s: {"rep": zl * 4 + mod4(xx + s)} for s in (1, 2, 3)}
    l_peer = {s: {"rep": mod4(zl + s) * 4 + xx} for s in (1, 2, 3)}

    barrier = pltpu.get_barrier_semaphore()
    peers = [sib] + list(y_peer.values()) + list(h_peer.values())
    if outer:
        peers += list(x_peer.values()) + list(l_peer.values())
    for peer in peers:
        pl.semaphore_signal(barrier, inc=1, device_id=peer, device_id_type=MESH)

    def blk(p, yy, cc, part=None):
        start = ((p * 4 + yy) * 2 + cc) * rows
        if part is None:
            return wbuf.at[pl.ds(pl.multiple_of(start, rows), rows), :]
        return wbuf.at[pl.ds(pl.multiple_of(start + part * half, half), half), :]

    own_copies = [
        (resid_hbm, x),
        (kv_hbm, kv),
        (gain_hbm, gain),
        (w_hbm, blk(h, y, c)),
        (delta_hbm, delta),
        (mom_hbm, mom),
        (par_hbm, par),
    ]
    loads = [pltpu.make_async_copy(a, b, sem_in.at[i]) for i, (a, b) in enumerate(own_copies)]
    for load in loads:
        load.start()

    pending = []

    def send(src, dst, ssem, rsem, peer):
        copy = pltpu.make_async_remote_copy(
            src_ref=src, dst_ref=dst, send_sem=ssem, recv_sem=rsem, device_id=peer, device_id_type=MESH
        )
        copy.start()
        pending.append(copy)

    def landed(dst, ssem, rsem, peer):
        pltpu.make_async_remote_copy(
            src_ref=dst, dst_ref=dst, send_sem=ssem, recv_sem=rsem, device_id=peer, device_id_type=MESH
        ).wait_recv()

    pl.semaphore_wait(barrier, len(peers))

    PART = (0, 1, 1, 0, 0, 1)
    WAY = (1, -1, 1, -1, 1, -1)

    def az_send(k):
        if k < 4:
            src = w_hbm.at[pl.ds(PART[k] * half, half), :]
            dst = blk(h, y, c, PART[k])
        else:
            src = dst = blk(mod4(h - WAY[k]), y, c, PART[k])
        send(src, dst, az_s.at[k], az_r.at[k], h_peer[WAY[k]])

    def az_wait(k):
        p = mod4(h - WAY[k] * (1 if k < 4 else 2))
        landed(blk(p, y, c, PART[k]), az_s.at[k], az_r.at[k], h_peer[WAY[k]])

    def ay_send(d, k):
        p = mod4(h + d)
        if k < 4:
            dst = blk(p, y, c, PART[k])
            src = w_hbm.at[pl.ds(PART[k] * half, half), :] if d == 0 else dst
        else:
            src = dst = blk(p, mod4(y - WAY[k]), c, PART[k])
        send(src, dst, ay_s.at[d, k], ay_r.at[d, k], y_peer[WAY[k]])

    def ay_wait(d, k):
        yy = mod4(y - WAY[k] * (1 if k < 4 else 2))
        landed(blk(mod4(h + d), yy, c, PART[k]), ay_s.at[d, k], ay_r.at[d, k], y_peer[WAY[k]])

    def as_send(d, r):
        b = blk(mod4(h + d), mod4(y + r), c)
        src = w_hbm if (d, r) == (0, 0) else b
        send(src, b, as_s.at[d, r], as_r.at[d, r], sib)

    def as_wait(d, r):
        landed(blk(mod4(h + d), mod4(y + r), 1 - c), as_s.at[d, r], as_r.at[d, r], sib)

    for k in (0, 1, 2, 3):
        az_send(k)
    for k in (0, 1, 2, 3):
        ay_send(0, k)
    loads[1].wait()
    send(kv, kv_sib, nt_s.at[4], nt_r.at[4], sib)
    as_send(0, 0)

    loads[0].wait()
    loads[2].wait()

    @pl.loop(0, tok // 32)
    def _(i):
        at = pl.ds(pl.multiple_of(i * 32, 32), 32)
        v = x[at, :].astype(F32)
        mean = jnp.mean(v * v, axis=-1, keepdims=True)
        scale[at, :] = jnp.broadcast_to(lax.rsqrt(mean + EPSILON), (32, LANES))

    def norm(d):
        p = mod4(h + d)

        @pl.loop(0, 4)
        def _(yy):
            lanes = pl.ds(pl.multiple_of((p * 4 + yy) * pair, pair), pair)
            unit = x[:, lanes].astype(F32) * scale[...]
            t = (unit * gain[0:1, lanes]).astype(BF16).T
            at = pl.ds(pl.multiple_of(yy * rows, rows), rows)
            nt[0, d, at, :] = t[:rows]
            nt[1, d, at, :] = t[rows:]

        send(nt.at[1 - c, d], nt_sib.at[d], nt_s.at[d], nt_r.at[d], sib)

    def partial(d):
        landed(nt_sib.at[d], nt_s.at[d], nt_r.at[d], sib)
        step = min(256, kvw)

        @pl.loop(0, kvw // step)
        def _(i):
            at = pl.ds(pl.multiple_of(i * step, step), step)
            t = jnp.dot(nt[c, d], kv[:, at], preferred_element_type=F32)
            t = t + jnp.dot(nt_sib[d], kv_sib[:, at], preferred_element_type=F32)
            pb[d, :, at] = t.astype(BF16)

        for k in (0, 1, 2, 3):
            ry_send(d, k)

    def piece(d, yy, part):
        return pl.ds(pl.multiple_of(mod4(yy) * rows + part * half, half), half)

    def ry_send(d, k):
        dest = y + (2 * WAY[k] if k < 2 else WAY[k])
        send(pb.at[d, piece(d, dest, PART[k]), :], ybuf.at[d, k], ry_s.at[d, k], ry_r.at[d, k], y_peer[WAY[k]])

    def ry_wait(d, k):
        landed(ybuf.at[d, k], ry_s.at[d, k], ry_r.at[d, k], y_peer[WAY[k]])

    def ry_mid(d):
        for k in (0, 1):
            ry_wait(d, k)
            at = piece(d, y + WAY[k], PART[k])
            pb[d, at, :] = (pb[d, at, :].astype(F32) + ybuf[d, k].astype(F32)).astype(BF16)
            ry_send(d, k + 4)

    def ry_end(d):
        for part, ks in ((0, (3, 4)), (1, (2, 5))):
            for k in ks:
                ry_wait(d, k)
            t = pb[d, piece(d, y, part), :].astype(F32)
            for k in ks:
                t = t + ybuf[d, k].astype(F32)
            yb[d, part] = t.astype(BF16)

    def rz_send(k):
        d = 2 if k < 2 else WAY[k] % 4
        send(yb.at[d, PART[k]], zbuf.at[k], rz_s.at[k], rz_r.at[k], h_peer[WAY[k]])

    def rz_wait(k):
        landed(zbuf.at[k], rz_s.at[k], rz_r.at[k], h_peer[WAY[k]])

    def rz_mid(k):
        rz_wait(k)
        d, part = WAY[k] % 4, PART[k]
        yb[d, part] = (yb[d, part].astype(F32) + zbuf[k].astype(F32)).astype(BF16)
        rz_send(k + 4)

    def rz_end():
        for part, ks in ((0, (3, 4)), (1, (2, 5))):
            for k in ks:
                rz_wait(k)
            t = yb[0, part].astype(F32)
            for k in ks:
                t = t + zbuf[k].astype(F32)
            gkv_out[part * half : (part + 1) * half, :] = t.astype(BF16)

    def chunk(d, r):
        j = mod4(h + d) * 4 + mod4(y + r)
        lanes = pl.ds(pl.multiple_of(j * pair, pair), pair)
        ng = lax.dot_general(kv[...], wbuf[lanes, :], (((1,), (1,)), ((), ())), preferred_element_type=F32)
        unit = x[:, lanes].astype(F32) * scale[...]
        gs[pl.ds(j, 1), :] = jnp.sum(ng * unit, axis=0, keepdims=True)
        g = ng * gain[0:1, lanes]
        acc[...] += g * unit
        gb[:, lanes] = g

    def plane(d):
        for r in (0, 3, 1, 2):
            as_wait(d, r)
            chunk(d, r)

    def outer_first():
        loads[4].wait()
        width = feat // 4
        for i in range(4):
            dl[i] = delta[:, i * width : (i + 1) * width].astype(BF16)
        for s in (1, 2, 3):
            send(dl.at[mod4(xx + s)], dx.at[s], ox_s.at[s], ox_r.at[s], x_peer[s])

    def outer_second():
        t = dl[xx].astype(F32)
        for s in (1, 2, 3):
            landed(dx.at[s], ox_s.at[s], ox_r.at[s], x_peer[s])
            t = t + dx[s].astype(F32)
        dz[zl] = t.astype(BF16)
        for s in (1, 2, 3):
            send(dz.at[zl], dz.at[zl], og_s.at[0, s], og_r.at[0, s], l_peer[s])

    def outer_third():
        for s in (1, 2, 3):
            landed(dz.at[mod4(zl - s)], og_s.at[0, s], og_r.at[0, s], l_peer[s])
        t = dz[0].astype(F32) + dz[1].astype(F32) + dz[2].astype(F32) + dz[3].astype(F32)
        dt[xx] = t.astype(BF16)
        for s in (1, 2, 3):
            send(dt.at[xx], dt.at[xx], og_s.at[1, s], og_r.at[1, s], x_peer[s])

    def outer_last():
        for s in (1, 2, 3):
            landed(dt.at[mod4(xx - s)], og_s.at[1, s], og_r.at[1, s], x_peer[s])
        loads[5].wait()
        loads[6].wait()
        width = feat // 4
        phase = jnp.full((1, LANES), sync_ref[0].astype(F32)) / ROUNDS
        rate = (OUTER_RATE * (1.0 + jnp.cos(jnp.pi * phase)) / 2.0)[0:1, 0:1]
        for i in range(4):
            at = slice(i * width, (i + 1) * width)
            mean = dt[i].astype(F32) * (1.0 / 16)
            fresh = NESTEROV_MU * mom[:, at] + mean
            nmom_out[:, at] = fresh
            npar_out[:, at] = par[:, at] - rate * (mean + NESTEROV_MU * fresh)

    acc[...] = jnp.zeros_like(acc)
    norm(2)
    norm(1)
    landed(kv_sib, nt_s.at[4], nt_r.at[4], sib)
    partial(2)
    for k in (0, 1):
        ay_wait(0, k)
        ay_send(0, k + 4)
    norm(3)
    partial(1)
    norm(0)
    partial(3)
    partial(0)
    if outer:
        outer_first()
    ry_mid(2)
    for k in (2, 3):
        ay_wait(0, k)
    as_send(0, 3)
    as_send(0, 1)
    loads[3].wait()
    az_wait(0)
    az_send(4)
    ay_send(3, 0)
    ay_send(3, 3)
    az_wait(1)
    az_send(5)
    ay_send(1, 1)
    ay_send(1, 2)
    ry_mid(1)
    ry_end(2)
    rz_send(0)
    rz_send(1)
    if outer:
        outer_second()
    ry_mid(3)
    ay_wait(0, 4)
    ay_wait(0, 5)
    as_send(0, 2)
    ry_mid(0)
    plane(0)
    az_wait(2)
    ay_send(3, 1)
    ay_send(3, 2)
    az_wait(3)
    ay_send(1, 0)
    ay_send(1, 3)
    as_send(3, 0)
    as_send(1, 0)
    ry_end(1)
    rz_send(2)
    ry_end(3)
    rz_send(3)
    if outer:
        outer_third()
    rz_mid(0)
    rz_mid(1)
    ry_end(0)
    az_wait(4)
    ay_send(2, 0)
    ay_send(2, 3)
    az_wait(5)
    ay_send(2, 1)
    ay_send(2, 2)
    as_send(2, 0)
    for k in (0, 1):
        ay_wait(3, k)
        ay_send(3, k + 4)
    for k in (0, 1):
        ay_wait(1, k)
        ay_send(1, k + 4)
    if outer:
        outer_last()
    for d in (3, 1):
        for k in (2, 3):
            ay_wait(d, k)
        as_send(d, 3)
        as_send(d, 1)
    for k in (0, 1):
        ay_wait(2, k)
        ay_send(2, k + 4)
    for d in (3, 1):
        for k in (4, 5):
            ay_wait(d, k)
        as_send(d, 2)
        plane(d)
    for k in (2, 3):
        ay_wait(2, k)
    as_send(2, 3)
    as_send(2, 1)
    for k in (4, 5):
        ay_wait(2, k)
    as_send(2, 2)
    plane(2)

    send(gs, gsib, gg_s.at[0], gg_r.at[0], sib)
    inner = jnp.sum(acc[...], axis=-1, keepdims=True) * (1.0 / feat)
    acc[...] = jnp.broadcast_to(inner, acc.shape)
    landed(gsib, gg_s.at[0], gg_r.at[0], sib)
    gy[y] = gs[...] + gsib[...]
    for s in (1, -1, 2):
        send(gy.at[y], gy.at[y], gg_s.at[2 + s], gg_r.at[2 + s], y_peer[s])

    outs = []
    block = min(64, tok)

    def final(i):
        at = slice(i * block, (i + 1) * block)
        sc, inn = scale[at, :], acc[at, :]
        for j in range(chunks):
            lanes = slice(j * pair, (j + 1) * pair)
            unit = x[at, lanes].astype(F32) * sc
            obuf[at, lanes] = (sc * (gb[at, lanes] - unit * inn)).astype(BF16)
        out = pltpu.make_async_copy(obuf.at[at, :], gin_hbm.at[at, :], sem_out.at[i])
        out.start()
        outs.append(out)

    n_final = tok // block
    for i in range(n_final):
        if i == n_final // 2:
            for s in (1, -1, 2):
                landed(gy.at[mod4(y - s)], gg_s.at[2 + s], gg_r.at[2 + s], y_peer[s])
            gz[h] = gy[0] + gy[1] + gy[2] + gy[3]
            for s in (1, -1, 2):
                send(gz.at[h], gz.at[h], gg_s.at[6 + s], gg_r.at[6 + s], h_peer[s])
        final(i)

    rz_end()
    for s in (1, -1, 2):
        landed(gz.at[mod4(h - s)], gg_s.at[6 + s], gg_r.at[6 + s], h_peer[s])
    total = gz[0] + gz[1] + gz[2] + gz[3]
    for j in range(chunks):
        ggain_out[0:1, j * pair : (j + 1) * pair] = total[j : j + 1, :]
    for copy in pending:
        copy.wait_send()
    for out in outs:
        out.wait()


def local(residual_in, norm_gain, kv_weight, kv_grad, outer_delta, outer_momentum, global_params, sync_index, outer=True):
    tok, feat = residual_in.shape[1:]
    rows, kvw = kv_weight.shape[1:]
    frag = outer_delta.shape[1]
    half, pair = rows // 2, 2 * rows
    chunks = feat // pair
    any_space = pl.BlockSpec(memory_space=pl.ANY)
    vmem = pl.BlockSpec(memory_space=pltpu.VMEM)
    dma = pltpu.SemaphoreType.DMA
    width = feat // 4
    grad_kv, grad_gain, grad_input, new_params, new_momentum = pl.pallas_call(
        functools.partial(kernel, (tok, feat, kvw, outer)),
        out_shape=(
            jax.ShapeDtypeStruct((rows, kvw), BF16),
            jax.ShapeDtypeStruct((1, feat), F32),
            jax.ShapeDtypeStruct((tok, feat), BF16),
            jax.ShapeDtypeStruct((frag, feat), F32),
            jax.ShapeDtypeStruct((frag, feat), F32),
        ),
        in_specs=[any_space] * 7 + [pl.BlockSpec(memory_space=pltpu.SMEM)],
        out_specs=(vmem, vmem, any_space, vmem, vmem),
        scratch_shapes=[
            pltpu.VMEM((tok, feat), BF16),
            pltpu.VMEM((1, feat), F32),
            pltpu.VMEM((feat, kvw), BF16),
            pltpu.VMEM((tok, kvw), BF16),
            pltpu.VMEM((tok, kvw), BF16),
            pltpu.VMEM((2, 4, 4 * rows, tok), BF16),
            pltpu.VMEM((4, 4 * rows, tok), BF16),
            pltpu.VMEM((4, 4 * rows, kvw), BF16),
            pltpu.VMEM((4, 6, half, kvw), BF16),
            pltpu.VMEM((4, 2, half, kvw), BF16),
            pltpu.VMEM((6, half, kvw), BF16),
            pltpu.VMEM((tok, LANES), F32),
            pltpu.VMEM((tok, LANES), F32),
            pltpu.VMEM((tok, feat), F32),
            pltpu.VMEM((tok, feat), BF16),
            pltpu.VMEM((chunks, pair), F32),
            pltpu.VMEM((chunks, pair), F32),
            pltpu.VMEM((4, chunks, pair), F32),
            pltpu.VMEM((4, chunks, pair), F32),
            pltpu.VMEM((frag, feat), F32),
            pltpu.VMEM((frag, feat), F32),
            pltpu.VMEM((frag, feat), F32),
            pltpu.VMEM((4, frag, width), BF16),
            pltpu.VMEM((4, frag, width), BF16),
            pltpu.VMEM((4, frag, width), BF16),
            pltpu.VMEM((4, frag, width), BF16),
            dma((7,)),
            dma((tok // min(64, tok),)),
            dma((6,)),
            dma((6,)),
            dma((4, 6)),
            dma((4, 6)),
            dma((4, 4)),
            dma((4, 4)),
            dma((5,)),
            dma((5,)),
            dma((4, 6)),
            dma((4, 6)),
            dma((6,)),
            dma((6,)),
            dma((4,)),
            dma((4,)),
            dma((2, 4)),
            dma((2, 4)),
            dma((9,)),
            dma((9,)),
        ],
        compiler_params=pltpu.CompilerParams(
            collective_id=0, has_side_effects=True, vmem_limit_bytes=56 * 1024 * 1024
        ),
    )(
        residual_in[0],
        norm_gain,
        kv_weight[0],
        kv_grad[0],
        outer_delta[0],
        outer_momentum,
        global_params,
        sync_index,
    )
    return (grad_kv[None], grad_gain, grad_input[None], new_params, new_momentum)


def solution(mesh):
    placed = (
        P("rep", "fsdp", None),
        P("rep", None),
        P("rep", "fsdp", None),
        P("rep", "fsdp", None),
        P("rep", "fsdp", None),
        P("fsdp", None),
        P("fsdp", None),
        P(),
    )
    return jax.shard_map(
        local,
        mesh=mesh,
        in_specs=placed,
        out_specs=(
            P("rep", "fsdp", None),
            P("rep", None),
            P("rep", "fsdp", None),
            P("fsdp", None),
            P("fsdp", None),
        ),
        check_vma=False,
    )
```

```python
import functools

import jax
import jax.numpy as jnp
from jax import lax
from jax.experimental import pallas as pl
from jax.experimental.pallas import tpu as pltpu
from jax.sharding import PartitionSpec as P

ROUNDS = 64
EPSILON = 1e-05
NESTEROV_MU = 0.9
OUTER_RATE = 0.7
MESH = pl.DeviceIdType.MESH
F32, BF16 = jnp.float32, jnp.bfloat16
LANES = 128


ORDER = (
    ("norm", 2),
    ("norm", 1),
    ("norm", 3),
    ("ay_fwd", 0, 4),
    ("ay_fwd", 0, 5),
    ("over", 0, 1),
    ("over", 0, 3),
    ("kv_here",),
    ("partial", 2),
    ("partial", 1),
    ("partial", 3),
    ("outer_first",),
    ("over", 0, 2),
    ("mul", 0, 0),
    ("mul", 0, 1),
    ("mul", 0, 3),
    ("mul", 0, 2),
    ("outer_second",),
    ("az_fwd", 4),
    ("az_fwd", 5),
    ("ry_mid", 2, 0),
    ("ry_mid", 2, 1),
    ("over", 1, 0),
    ("outer_third",),
    ("over", 3, 0),
    ("ry_mid", 1, 0),
    ("ry_mid", 1, 1),
    ("ry_mid", 3, 0),
    ("ry_mid", 3, 1),
    ("ay_first", 3, 0),
    ("ay_first", 1, 1),
    ("outer_last",),
    ("ry_end", 2, 1),
    ("ry_end", 2, 0),
    ("ay_first", 1, 0),
    ("rz_send", 0),
    ("rz_send", 1),
    ("mul", 3, 0),
    ("ry_end", 1, 0),
    ("ry_end", 1, 1),
    ("rz_send", 2),
    ("ay_first", 3, 1),
    ("over", 2, 0),
    ("ry_end", 3, 0),
    ("ry_end", 3, 1),
    ("ay_fwd", 1, 5),
    ("ay_fwd", 3, 4),
    ("norm", 0),
    ("ay_fwd", 1, 4),
    ("over", 1, 1),
    ("over", 1, 3),
    ("ay_first", 2, 0),
    ("ay_first", 2, 1),
    ("rz_send", 3),
    ("mul", 1, 0),
    ("mul", 2, 0),
    ("over", 3, 3),
    ("ay_fwd", 3, 5),
    ("over", 3, 1),
    ("mul", 1, 1),
    ("partial", 0),
    ("rz_mid", 1),
    ("mul", 1, 3),
    ("mul", 3, 1),
    ("mul", 3, 3),
    ("rz_mid", 0),
    ("ay_fwd", 2, 5),
    ("over", 2, 1),
    ("over", 1, 2),
    ("ay_fwd", 2, 4),
    ("over", 2, 3),
    ("over", 3, 2),
    ("mul", 2, 1),
    ("mul", 1, 2),
    ("mul", 2, 3),
    ("ry_mid", 0, 0),
    ("ry_mid", 0, 1),
    ("mul", 3, 2),
    ("over", 2, 2),
    ("mul", 2, 2),
    ("ry_end", 0, 0),
    ("ry_end", 0, 1),
)
LATE = (
    ("rz_end", 0),
    ("rz_end", 1),
    ("gain_send",),
)


def kernel(
    sizes,
    resid_hbm,
    gain_hbm,
    w_hbm,
    kv_hbm,
    delta_hbm,
    mom_hbm,
    par_hbm,
    sync_ref,
    gkv_out,
    ggain_out,
    gin_hbm,
    npar_out,
    nmom_out,
    x,
    gain,
    wbuf,
    kv,
    kv_sib,
    nt,
    nt_sib,
    pb,
    ybuf,
    yb,
    zbuf,
    scale,
    acc,
    gb,
    obuf,
    gfold,
    gall,
    delta,
    mom,
    par,
    dl,
    dx,
    dz,
    dt,
    sem_in,
    sem_out,
    az_s,
    az_r,
    ay_s,
    ay_r,
    as_s,
    as_r,
    nt_s,
    nt_r,
    ry_s,
    ry_r,
    rz_s,
    rz_r,
    ox_s,
    ox_r,
    og_s,
    og_r,
    gg_s,
    gg_r,
):
    tok, feat, kvw, outer = sizes
    rows = w_hbm.shape[0]
    half = rows // 2
    pair = 2 * rows
    chunks = feat // pair
    f = lax.axis_index("fsdp")
    c = lax.rem(f, 2)
    y = lax.rem(lax.div(f, 2), 4)
    h = lax.div(f, 8)
    rep = lax.axis_index("rep")
    xx = lax.rem(rep, 4)
    zl = lax.div(rep, 4)

    def mod4(v):
        return lax.rem(v + 8, 4)

    def inside(hh, yy, cc):
        return {"fsdp": (hh * 4 + yy) * 2 + cc}

    sib = inside(h, y, 1 - c)
    y_peer = {s: inside(h, mod4(y + s), c) for s in (1, -1, 2)}
    h_peer = {s: inside(mod4(h + s), y, c) for s in (1, -1, 2)}
    x_peer = {s: {"rep": zl * 4 + mod4(xx + s)} for s in (1, 2, 3)}
    l_peer = {s: {"rep": mod4(zl + s) * 4 + xx} for s in (1, 2, 3)}

    barrier = pltpu.get_barrier_semaphore()
    size = 2 * chunks
    f_peer = {s: {"fsdp": lax.rem(f + s, size)} for s in range(1, size)}
    peers = list(f_peer.values())
    if outer:
        peers += list(x_peer.values()) + list(l_peer.values())
    for peer in peers:
        pl.semaphore_signal(barrier, inc=1, device_id=peer, device_id_type=MESH)

    def blk(p, yy, cc, part=None):
        start = ((p * 4 + yy) * 2 + cc) * rows
        if part is None:
            return wbuf.at[pl.ds(pl.multiple_of(start, rows), rows), :]
        return wbuf.at[pl.ds(pl.multiple_of(start + part * half, half), half), :]

    own_copies = [
        (resid_hbm, x),
        (kv_hbm, kv),
        (gain_hbm, gain),
        (w_hbm, blk(h, y, c)),
        (delta_hbm, delta),
        (mom_hbm, mom),
        (par_hbm, par),
    ]
    loads = [pltpu.make_async_copy(a, b, sem_in.at[i]) for i, (a, b) in enumerate(own_copies)]
    for i in (3, 1, 0, 2, 4, 5, 6):
        loads[i].start()

    pending = []

    def send(src, dst, ssem, rsem, peer):
        copy = pltpu.make_async_remote_copy(
            src_ref=src, dst_ref=dst, send_sem=ssem, recv_sem=rsem, device_id=peer, device_id_type=MESH
        )
        copy.start()
        pending.append(copy)

    def landed(dst, ssem, rsem, peer):
        pltpu.make_async_remote_copy(
            src_ref=dst, dst_ref=dst, send_sem=ssem, recv_sem=rsem, device_id=peer, device_id_type=MESH
        ).wait_recv()

    loads[3].wait()
    pl.semaphore_wait(barrier, len(peers))

    seen = set()

    def need(wait, *key):
        if (wait, key) not in seen:
            seen.add((wait, key))
            wait(*key)

    PART = (0, 1, 1, 0, 0, 1)
    WAY = (1, -1, 1, -1, 1, -1)

    def az_send(k):
        if k < 4:
            src = dst = blk(h, y, c, PART[k])
        else:
            src = dst = blk(mod4(h - WAY[k]), y, c, PART[k])
        send(src, dst, az_s.at[k], az_r.at[k], h_peer[WAY[k]])

    def az_wait(k):
        p = mod4(h - WAY[k] * (1 if k < 4 else 2))
        landed(blk(p, y, c, PART[k]), az_s.at[k], az_r.at[k], h_peer[WAY[k]])

    def ay_send(d, k):
        p = mod4(h + d)
        if k < 4:
            src = dst = blk(p, y, c, PART[k])
        else:
            src = dst = blk(p, mod4(y - WAY[k]), c, PART[k])
        send(src, dst, ay_s.at[d, k], ay_r.at[d, k], y_peer[WAY[k]])

    def ay_wait(d, k):
        yy = mod4(y - WAY[k] * (1 if k < 4 else 2))
        landed(blk(mod4(h + d), yy, c, PART[k]), ay_s.at[d, k], ay_r.at[d, k], y_peer[WAY[k]])

    def as_send(d, r):
        b = blk(mod4(h + d), mod4(y + r), c)
        send(b, b, as_s.at[d, r], as_r.at[d, r], sib)

    def as_wait(d, r):
        landed(blk(mod4(h + d), mod4(y + r), 1 - c), as_s.at[d, r], as_r.at[d, r], sib)

    for k in (0, 1, 2, 3):
        az_send(k)
    for k in (0, 1, 2, 3):
        ay_send(0, k)
    loads[1].wait()
    send(kv, kv_sib, nt_s.at[4], nt_r.at[4], sib)
    as_send(0, 0)

    loads[0].wait()
    loads[2].wait()

    @pl.loop(0, tok // 32)
    def _(i):
        at = pl.ds(pl.multiple_of(i * 32, 32), 32)
        v = x[at, :].astype(F32)
        mean = jnp.mean(v * v, axis=-1, keepdims=True)
        scale[at, :] = jnp.broadcast_to(lax.rsqrt(mean + EPSILON), (32, LANES))

    def norm(d):
        p = mod4(h + d)

        @pl.loop(0, 4)
        def _(yy):
            lanes = pl.ds(pl.multiple_of((p * 4 + yy) * pair, pair), pair)
            unit = x[:, lanes].astype(F32) * scale[...]
            t = (unit * gain[0:1, lanes]).astype(BF16).T
            at = pl.ds(pl.multiple_of(yy * rows, rows), rows)
            nt[0, d, at, :] = t[:rows]
            nt[1, d, at, :] = t[rows:]

        send(nt.at[1 - c, d], nt_sib.at[d], nt_s.at[d], nt_r.at[d], sib)

    def partial(d):
        landed(nt_sib.at[d], nt_s.at[d], nt_r.at[d], sib)
        step = min(256, kvw)

        @pl.loop(0, kvw // step)
        def _(i):
            at = pl.ds(pl.multiple_of(i * step, step), step)
            t = jnp.dot(nt[c, d], kv[:, at], preferred_element_type=F32)
            t = t + jnp.dot(nt_sib[d], kv_sib[:, at], preferred_element_type=F32)
            pb[d, :, at] = t.astype(BF16)

        for k in (0, 1, 2, 3):
            ry_send(d, k)

    def piece(d, yy, part):
        return pl.ds(pl.multiple_of(mod4(yy) * rows + part * half, half), half)

    def ry_send(d, k):
        dest = y + (2 * WAY[k] if k < 2 else WAY[k])
        send(pb.at[d, piece(d, dest, PART[k]), :], ybuf.at[d, k], ry_s.at[d, k], ry_r.at[d, k], y_peer[WAY[k]])

    def ry_wait(d, k):
        landed(ybuf.at[d, k], ry_s.at[d, k], ry_r.at[d, k], y_peer[WAY[k]])

    ENDS = ((3, 4), (2, 5))

    def ry_mid(d, k):
        need(ry_wait, d, k)
        at = piece(d, y + WAY[k], PART[k])
        pb[d, at, :] = (pb[d, at, :].astype(F32) + ybuf[d, k].astype(F32)).astype(BF16)
        ry_send(d, k + 4)

    def ry_end(d, part):
        t = pb[d, piece(d, y, part), :].astype(F32)
        for k in ENDS[part]:
            need(ry_wait, d, k)
            t = t + ybuf[d, k].astype(F32)
        yb[d, part] = t.astype(BF16)

    def rz_send(k):
        d = 2 if k < 2 else WAY[k] % 4
        send(yb.at[d, PART[k]], zbuf.at[k], rz_s.at[k], rz_r.at[k], h_peer[WAY[k]])

    def rz_wait(k):
        landed(zbuf.at[k], rz_s.at[k], rz_r.at[k], h_peer[WAY[k]])

    def rz_mid(k):
        need(rz_wait, k)
        d, part = WAY[k] % 4, PART[k]
        yb[d, part] = (yb[d, part].astype(F32) + zbuf[k].astype(F32)).astype(BF16)
        rz_send(k + 4)

    def rz_end(part):
        t = yb[0, part].astype(F32)
        for k in ENDS[part]:
            need(rz_wait, k)
            t = t + zbuf[k].astype(F32)
        gkv_out[part * half : (part + 1) * half, :] = t.astype(BF16)
        t = t * blk(h, y, c, part)[...].astype(F32)
        fold = t[:, :LANES]
        for i in range(1, kvw // LANES):
            fold = fold + t[:, i * LANES : (i + 1) * LANES]
        gfold[pl.ds(pl.multiple_of(c * rows + part * half, half), half), :] = fold

    def gain_send():
        lanes = pl.ds(pl.multiple_of((h * 4 + y) * pair, pair), pair)
        gall[f] = jnp.sum(gfold[...].T, axis=0, keepdims=True) / gain[0:1, lanes]
        for s in range(1, size):
            send(gall.at[f], gall.at[f], gg_s.at[s], gg_r.at[s], f_peer[s])

    def gain_end():
        for s in range(1, size):
            landed(gall.at[lax.rem(f + size - s, size)], gg_s.at[s], gg_r.at[s], f_peer[s])
        for j in range(chunks):
            ggain_out[0:1, j * pair : (j + 1) * pair] = gall[2 * j] + gall[2 * j + 1]

    def chunk(d, r):
        j = mod4(h + d) * 4 + mod4(y + r)
        lanes = pl.ds(pl.multiple_of(j * pair, pair), pair)
        ng = lax.dot_general(kv[...], wbuf[lanes, :], (((1,), (1,)), ((), ())), preferred_element_type=F32)
        unit = x[:, lanes].astype(F32) * scale[...]
        g = ng * gain[0:1, lanes]
        acc[...] += g * unit
        gb[:, lanes] = g

    def outer_first():
        loads[4].wait()
        width = feat // 4
        for i in range(4):
            dl[i] = delta[:, i * width : (i + 1) * width].astype(BF16)
        for s in (1, 2, 3):
            send(dl.at[mod4(xx + s)], dx.at[s], ox_s.at[s], ox_r.at[s], x_peer[s])

    def outer_second():
        t = dl[xx].astype(F32)
        for s in (1, 2, 3):
            landed(dx.at[s], ox_s.at[s], ox_r.at[s], x_peer[s])
            t = t + dx[s].astype(F32)
        dz[zl] = t.astype(BF16)
        for s in (1, 2, 3):
            send(dz.at[zl], dz.at[zl], og_s.at[0, s], og_r.at[0, s], l_peer[s])

    def outer_third():
        for s in (1, 2, 3):
            landed(dz.at[mod4(zl - s)], og_s.at[0, s], og_r.at[0, s], l_peer[s])
        t = dz[0].astype(F32) + dz[1].astype(F32) + dz[2].astype(F32) + dz[3].astype(F32)
        dt[xx] = t.astype(BF16)
        for s in (1, 2, 3):
            send(dt.at[xx], dt.at[xx], og_s.at[1, s], og_r.at[1, s], x_peer[s])

    def outer_last():
        for s in (1, 2, 3):
            landed(dt.at[mod4(xx - s)], og_s.at[1, s], og_r.at[1, s], x_peer[s])
        loads[5].wait()
        loads[6].wait()
        width = feat // 4
        phase = jnp.full((1, LANES), sync_ref[0].astype(F32)) / ROUNDS
        rate = (OUTER_RATE * (1.0 + jnp.cos(jnp.pi * phase)) / 2.0)[0:1, 0:1]
        for i in range(4):
            at = slice(i * width, (i + 1) * width)
            mean = dt[i].astype(F32) * (1.0 / 16)
            fresh = NESTEROV_MU * mom[:, at] + mean
            nmom_out[:, at] = fresh
            npar_out[:, at] = par[:, at] - rate * (mean + NESTEROV_MU * fresh)

    def az_fwd(k):
        need(az_wait, k - 4)
        az_send(k)

    def ay_first(d, part):
        need(az_wait, {(3, 0): 0, (1, 1): 1, (3, 1): 2, (1, 0): 3, (2, 0): 4, (2, 1): 5}[d, part])
        for k in ((0, 3), (1, 2))[part]:
            ay_send(d, k)

    def ay_fwd(d, k):
        need(ay_wait, d, k - 4)
        ay_send(d, k)

    def over(d, r):
        if r == 0:
            for k in {0: (), 1: (1, 3), 2: (4, 5), 3: (0, 2)}[d]:
                need(az_wait, k)
        else:
            for k in {3: (0, 2), 1: (1, 3), 2: (4, 5)}[r]:
                need(ay_wait, d, k)
        as_send(d, r)

    def mul(d, r):
        need(as_wait, d, r)
        chunk(d, r)

    acc[...] = jnp.zeros_like(acc)
    gfold[...] = jnp.zeros_like(gfold)
    kv_here = lambda: landed(kv_sib, nt_s.at[4], nt_r.at[4], sib)
    tasks = dict(
        norm=norm, kv_here=kv_here, partial=partial, az_fwd=az_fwd, ay_first=ay_first, ay_fwd=ay_fwd, over=over,
        mul=mul, ry_mid=ry_mid, ry_end=ry_end, rz_send=rz_send, rz_mid=rz_mid, rz_end=rz_end, gain_send=gain_send,
        outer_first=outer_first, outer_second=outer_second, outer_third=outer_third, outer_last=outer_last,
    )
    for name, *key in ORDER:
        if outer or not name.startswith("outer"):
            tasks[name](*key)
    inner = jnp.sum(acc[...], axis=-1, keepdims=True) * (1.0 / feat)
    acc[...] = jnp.broadcast_to(inner, acc.shape)

    outs = []
    block = min(64, tok)

    def final(i):
        at = slice(i * block, (i + 1) * block)
        sc, inn = scale[at, :], acc[at, :]
        for j in range(chunks):
            lanes = slice(j * pair, (j + 1) * pair)
            unit = x[at, lanes].astype(F32) * sc
            obuf[at, lanes] = (sc * (gb[at, lanes] - unit * inn)).astype(BF16)
        out = pltpu.make_async_copy(obuf.at[at, :], gin_hbm.at[at, :], sem_out.at[i])
        out.start()
        outs.append(out)

    n_final = tok // block
    for i in range(n_final):
        final(i)

    for name, *key in LATE:
        tasks[name](*key)
    gain_end()
    for copy in pending:
        copy.wait_send()
    for out in outs:
        out.wait()


def hand_on(*refs):
    n = 5
    ins, outs, stages, sems = refs[:n], refs[n : 2 * n], refs[2 * n : 3 * n], refs[3 * n]
    loads, stores = [], []
    for a, stage, b in zip(ins, stages, outs):
        split = 4 if a.shape[0] >= 256 else 1
        size = a.shape[0] // split
        for i in range(split):
            at = pl.ds(i * size, size)
            loads.append(pltpu.make_async_copy(a.at[at, :], stage.at[at, :], sems.at[0, len(loads)]))
            stores.append(pltpu.make_async_copy(stage.at[at, :], b.at[at, :], sems.at[1, len(stores)]))
    for load in loads:
        load.start()
    for load, store in zip(loads, stores):
        load.wait()
        store.start()
    for store in stores:
        store.wait()


def local(residual_in, norm_gain, kv_weight, kv_grad, outer_delta, outer_momentum, global_params, sync_index, outer=True):
    tok, feat = residual_in.shape[1:]
    rows, kvw = kv_weight.shape[1:]
    frag = outer_delta.shape[1]
    half, pair = rows // 2, 2 * rows
    chunks = feat // pair
    any_space = pl.BlockSpec(memory_space=pl.ANY)
    vmem = pl.BlockSpec(memory_space=pltpu.VMEM)
    dma = pltpu.SemaphoreType.DMA
    width = feat // 4
    results = pl.pallas_call(
        functools.partial(kernel, (tok, feat, kvw, outer)),
        out_shape=(
            jax.ShapeDtypeStruct((rows, kvw), BF16),
            jax.ShapeDtypeStruct((1, feat), F32),
            jax.ShapeDtypeStruct((tok, feat), BF16),
            jax.ShapeDtypeStruct((frag, feat), F32),
            jax.ShapeDtypeStruct((frag, feat), F32),
        ),
        in_specs=[any_space] * 7 + [pl.BlockSpec(memory_space=pltpu.SMEM)],
        out_specs=(vmem, vmem, any_space, vmem, vmem),
        scratch_shapes=[
            pltpu.VMEM((tok, feat), BF16),
            pltpu.VMEM((1, feat), F32),
            pltpu.VMEM((feat, kvw), BF16),
            pltpu.VMEM((tok, kvw), BF16),
            pltpu.VMEM((tok, kvw), BF16),
            pltpu.VMEM((2, 4, 4 * rows, tok), BF16),
            pltpu.VMEM((4, 4 * rows, tok), BF16),
            pltpu.VMEM((4, 4 * rows, kvw), BF16),
            pltpu.VMEM((4, 6, half, kvw), BF16),
            pltpu.VMEM((4, 2, half, kvw), BF16),
            pltpu.VMEM((6, half, kvw), BF16),
            pltpu.VMEM((tok, LANES), F32),
            pltpu.VMEM((tok, LANES), F32),
            pltpu.VMEM((tok, feat), F32),
            pltpu.VMEM((tok, feat), BF16),
            pltpu.VMEM((pair, LANES), F32),
            pltpu.VMEM((2 * chunks, 1, pair), F32),
            pltpu.VMEM((frag, feat), F32),
            pltpu.VMEM((frag, feat), F32),
            pltpu.VMEM((frag, feat), F32),
            pltpu.VMEM((4, frag, width), BF16),
            pltpu.VMEM((4, frag, width), BF16),
            pltpu.VMEM((4, frag, width), BF16),
            pltpu.VMEM((4, frag, width), BF16),
            dma((7,)),
            dma((tok // min(64, tok),)),
            dma((6,)),
            dma((6,)),
            dma((4, 6)),
            dma((4, 6)),
            dma((4, 4)),
            dma((4, 4)),
            dma((5,)),
            dma((5,)),
            dma((4, 6)),
            dma((4, 6)),
            dma((6,)),
            dma((6,)),
            dma((4,)),
            dma((4,)),
            dma((2, 4)),
            dma((2, 4)),
            dma((2 * chunks,)),
            dma((2 * chunks,)),
        ],
        compiler_params=pltpu.CompilerParams(
            collective_id=0, has_side_effects=True, vmem_limit_bytes=56 * 1024 * 1024
        ),
    )(
        residual_in[0],
        norm_gain,
        kv_weight[0],
        kv_grad[0],
        outer_delta[0],
        outer_momentum,
        global_params,
        sync_index,
    )
    grad_kv, grad_gain, grad_input, new_params, new_momentum = pl.pallas_call(
        hand_on,
        out_shape=tuple(jax.ShapeDtypeStruct(r.shape, r.dtype) for r in results),
        in_specs=[any_space] * 5,
        out_specs=(any_space,) * 5,
        scratch_shapes=[pltpu.VMEM(r.shape, r.dtype) for r in results] + [dma((2, 8))],
        compiler_params=pltpu.CompilerParams(vmem_limit_bytes=60 * 1024 * 1024),
    )(*results)
    return (grad_kv[None], grad_gain, grad_input[None], new_params, new_momentum)


def solution(mesh):
    placed = (
        P("rep", "fsdp", None),
        P("rep", None),
        P("rep", "fsdp", None),
        P("rep", "fsdp", None),
        P("rep", "fsdp", None),
        P("fsdp", None),
        P("fsdp", None),
        P(),
    )
    return jax.shard_map(
        local,
        mesh=mesh,
        in_specs=placed,
        out_specs=(
            P("rep", "fsdp", None),
            P("rep", None),
            P("rep", "fsdp", None),
            P("fsdp", None),
            P("fsdp", None),
        ),
        check_vma=False,
    )
```

```python
import functools

import jax
import jax.numpy as jnp
from jax import lax
from jax.experimental import pallas as pl
from jax.experimental.pallas import tpu as pltpu
from jax.sharding import PartitionSpec as P

ROUNDS = 64
EPSILON = 1e-05
NESTEROV_MU = 0.9
OUTER_RATE = 0.7
MESH = pl.DeviceIdType.MESH
F32, BF16 = jnp.float32, jnp.bfloat16
LANES = 128


ORDER = (
    ("norm", 2),
    ("norm", 1),
    ("mul", 0, 0),
    ("ay_fwd", 0, 4),
    ("ay_fwd", 0, 5),
    ("over", 0, 1),
    ("over", 0, 3),
    ("kv_here",),
    ("partial", 2),
    ("outer_first",),
    ("partial", 1),
    ("norm", 3),
    ("over", 0, 2),
    ("mul", 0, 1),
    ("mul", 0, 3),
    ("outer_second",),
    ("mul", 0, 2),
    ("partial", 3),
    ("ry_mid", 2, 0),
    ("ry_mid", 2, 1),
    ("norm", 0),
    ("outer_third",),
    ("az_fwd", 4),
    ("az_fwd", 5),
    ("over", 1, 0),
    ("over", 3, 0),
    ("ry_mid", 1, 0),
    ("ry_mid", 1, 1),
    ("partial", 0),
    ("outer_last",),
    ("ry_mid", 3, 1),
    ("ry_mid", 3, 0),
    ("mul", 1, 0),
    ("mul", 3, 0),
    ("ry_end", 2, 0),
    ("rz_send", 0),
    ("ry_end", 2, 1),
    ("rz_send", 1),
    ("ay_first", 2, 1),
    ("over", 2, 0),
    ("ry_end", 1, 0),
    ("ry_end", 1, 1),
    ("ay_first", 3, 0),
    ("ay_first", 1, 1),
    ("rz_send", 2),
    ("gain_part", 1, 0),
    ("gain_part", 1, 1),
    ("gain_part", 2, 0),
    ("ry_mid", 0, 0),
    ("ry_mid", 0, 1),
    ("gain_part", 2, 1),
    ("mul", 2, 0),
    ("ry_end", 3, 0),
    ("ay_first", 2, 0),
    ("ay_first", 3, 1),
    ("rz_send", 3),
    ("ry_end", 3, 1),
    ("gain_part", 3, 0),
    ("gain_part", 3, 1),
    ("rz_mid", 1),
    ("ay_fwd", 2, 5),
    ("ay_first", 1, 0),
    ("rz_mid", 0),
    ("ay_fwd", 3, 4),
    ("ry_end", 0, 0),
    ("gain_part", 0, 0),
    ("ry_end", 0, 1),
    ("gain_part", 0, 1),
    ("gain_send",),
    ("ay_fwd", 2, 4),
    ("over", 2, 3),
    ("over", 3, 3),
    ("over", 2, 1),
    ("ay_fwd", 3, 5),
    ("over", 3, 1),
    ("ay_fwd", 1, 4),
    ("ay_fwd", 1, 5),
    ("over", 1, 3),
    ("mul", 2, 3),
    ("over", 1, 1),
    ("mul", 2, 1),
    ("mul", 3, 1),
    ("mul", 3, 3),
    ("mul", 1, 3),
    ("over", 2, 2),
    ("over", 3, 2),
    ("mul", 1, 1),
    ("gain_pass",),
    ("over", 1, 2),
    ("mul", 2, 2),
    ("mul", 3, 2),
    ("rz_end", 0),
    ("rz_end", 1),
    ("mul", 1, 2),
)
LATE = (
    ("gain_end",),
)


def kernel(
    sizes,
    resid_hbm,
    gain_hbm,
    w_hbm,
    kv_hbm,
    delta_hbm,
    mom_hbm,
    par_hbm,
    sync_ref,
    gkv_hbm,
    ggain_hbm,
    gin_hbm,
    npar_hbm,
    nmom_hbm,
    x,
    gain,
    wbuf,
    kv,
    kv_sib,
    nt,
    nt_sib,
    pb,
    ybuf,
    yb,
    zbuf,
    scale,
    acc,
    gb,
    obuf,
    gkv,
    ggain,
    npar,
    nmom,
    gfold,
    gz,
    gall,
    delta,
    mom,
    par,
    dl,
    dx,
    dz,
    dt,
    sem_in,
    sem_out,
    az_s,
    az_r,
    ay_s,
    ay_r,
    as_s,
    as_r,
    nt_s,
    nt_r,
    ry_s,
    ry_r,
    rz_s,
    rz_r,
    ox_s,
    ox_r,
    og_s,
    og_r,
    gg_s,
    gg_r,
):
    tok, feat, kvw, outer = sizes
    rows = w_hbm.shape[0]
    half = rows // 2
    pair = 2 * rows
    chunks = feat // pair
    f = lax.axis_index("fsdp")
    c = lax.rem(f, 2)
    y = lax.rem(lax.div(f, 2), 4)
    h = lax.div(f, 8)
    rep = lax.axis_index("rep")
    xx = lax.rem(rep, 4)
    zl = lax.div(rep, 4)

    def mod4(v):
        return lax.rem(v + 8, 4)

    def inside(hh, yy, cc):
        return {"fsdp": (hh * 4 + yy) * 2 + cc}

    sib = inside(h, y, 1 - c)
    y_peer = {s: inside(h, mod4(y + s), c) for s in (1, -1, 2)}
    h_peer = {s: inside(mod4(h + s), y, c) for s in (1, -1, 2)}
    x_peer = {s: {"rep": zl * 4 + mod4(xx + s)} for s in (1, 2, 3)}
    l_peer = {s: {"rep": mod4(zl + s) * 4 + xx} for s in (1, 2, 3)}

    barrier = pltpu.get_barrier_semaphore()
    near = [sib] + [inside(h, mod4(y + s), cc) for s in (1, -1, 2) for cc in (c, 1 - c)]
    near_from = near[:1] + [inside(h, mod4(y - s), cc) for s in (1, -1, 2) for cc in (c, 1 - c)]
    peers = near + list(h_peer.values())
    if outer:
        peers += list(x_peer.values()) + list(l_peer.values())
    for peer in peers:
        pl.semaphore_signal(barrier, inc=1, device_id=peer, device_id_type=MESH)

    def blk(p, yy, cc, part=None):
        start = ((p * 4 + yy) * 2 + cc) * rows
        if part is None:
            return wbuf.at[pl.ds(pl.multiple_of(start, rows), rows), :]
        return wbuf.at[pl.ds(pl.multiple_of(start + part * half, half), half), :]

    own_copies = [
        (resid_hbm, x),
        (kv_hbm, kv),
        (gain_hbm, gain),
        (w_hbm, blk(h, y, c)),
        (delta_hbm, delta),
        (mom_hbm, mom),
        (par_hbm, par),
    ]
    loads = [pltpu.make_async_copy(a, b, sem_in.at[i]) for i, (a, b) in enumerate(own_copies)]
    for i in (3, 1, 0, 2, 4, 5, 6):
        loads[i].start()

    outs = []

    def give(src, dst):
        out = pltpu.make_async_copy(src, dst, sem_out.at[len(outs)])
        out.start()
        outs.append(out)

    pending = []

    def send(src, dst, ssem, rsem, peer):
        copy = pltpu.make_async_remote_copy(
            src_ref=src, dst_ref=dst, send_sem=ssem, recv_sem=rsem, device_id=peer, device_id_type=MESH
        )
        copy.start()
        pending.append(copy)

    def landed(dst, ssem, rsem, peer):
        pltpu.make_async_remote_copy(
            src_ref=dst, dst_ref=dst, send_sem=ssem, recv_sem=rsem, device_id=peer, device_id_type=MESH
        ).wait_recv()

    loads[3].wait()
    pl.semaphore_wait(barrier, len(peers))

    seen = set()

    def need(wait, *key):
        if (wait, key) not in seen:
            seen.add((wait, key))
            wait(*key)

    PART = (0, 1, 1, 0, 0, 1)
    WAY = (1, -1, 1, -1, 1, -1)

    def az_send(k):
        if k < 4:
            src = dst = blk(h, y, c, PART[k])
        else:
            src = dst = blk(mod4(h - WAY[k]), y, c, PART[k])
        send(src, dst, az_s.at[k], az_r.at[k], h_peer[WAY[k]])

    def az_wait(k):
        p = mod4(h - WAY[k] * (1 if k < 4 else 2))
        landed(blk(p, y, c, PART[k]), az_s.at[k], az_r.at[k], h_peer[WAY[k]])

    def ay_send(d, k):
        p = mod4(h + d)
        if k < 4:
            src = dst = blk(p, y, c, PART[k])
        else:
            src = dst = blk(p, mod4(y - WAY[k]), c, PART[k])
        send(src, dst, ay_s.at[d, k], ay_r.at[d, k], y_peer[WAY[k]])

    def ay_wait(d, k):
        yy = mod4(y - WAY[k] * (1 if k < 4 else 2))
        landed(blk(mod4(h + d), yy, c, PART[k]), ay_s.at[d, k], ay_r.at[d, k], y_peer[WAY[k]])

    def as_send(d, r):
        b = blk(mod4(h + d), mod4(y + r), c)
        send(b, b, as_s.at[d, r], as_r.at[d, r], sib)

    def as_wait(d, r):
        landed(blk(mod4(h + d), mod4(y + r), 1 - c), as_s.at[d, r], as_r.at[d, r], sib)

    for k in (0, 1, 2, 3):
        az_send(k)
    for k in (0, 1, 2, 3):
        ay_send(0, k)
    loads[1].wait()
    send(kv, kv_sib, nt_s.at[4], nt_r.at[4], sib)
    as_send(0, 0)

    loads[0].wait()
    loads[2].wait()

    @pl.loop(0, tok // 32)
    def _(i):
        at = pl.ds(pl.multiple_of(i * 32, 32), 32)
        v = x[at, :].astype(F32)
        mean = jnp.mean(v * v, axis=-1, keepdims=True)
        scale[at, :] = jnp.broadcast_to(lax.rsqrt(mean + EPSILON), (32, LANES))

    def norm(d):
        p = mod4(h + d)

        @pl.loop(0, 4)
        def _(yy):
            lanes = pl.ds(pl.multiple_of((p * 4 + yy) * pair, pair), pair)
            unit = x[:, lanes].astype(F32) * scale[...]
            t = (unit * gain[0:1, lanes]).astype(BF16).T
            at = pl.ds(pl.multiple_of(yy * rows, rows), rows)
            nt[0, d, at, :] = t[:rows]
            nt[1, d, at, :] = t[rows:]

        send(nt.at[1 - c, d], nt_sib.at[d], nt_s.at[d], nt_r.at[d], sib)

    def partial(d):
        landed(nt_sib.at[d], nt_s.at[d], nt_r.at[d], sib)
        step = min(256, kvw)

        @pl.loop(0, kvw // step)
        def _(i):
            at = pl.ds(pl.multiple_of(i * step, step), step)
            t = jnp.dot(nt[c, d], kv[:, at], preferred_element_type=F32)
            t = t + jnp.dot(nt_sib[d], kv_sib[:, at], preferred_element_type=F32)
            pb[d, :, at] = t.astype(BF16)

        for k in (0, 1, 2, 3):
            ry_send(d, k)

    def piece(d, yy, part):
        return pl.ds(pl.multiple_of(mod4(yy) * rows + part * half, half), half)

    def ry_send(d, k):
        dest = y + (2 * WAY[k] if k < 2 else WAY[k])
        send(pb.at[d, piece(d, dest, PART[k]), :], ybuf.at[d, k], ry_s.at[d, k], ry_r.at[d, k], y_peer[WAY[k]])

    def ry_wait(d, k):
        landed(ybuf.at[d, k], ry_s.at[d, k], ry_r.at[d, k], y_peer[WAY[k]])

    ENDS = ((3, 4), (2, 5))

    def ry_mid(d, k):
        need(ry_wait, d, k)
        at = piece(d, y + WAY[k], PART[k])
        pb[d, at, :] = (pb[d, at, :].astype(F32) + ybuf[d, k].astype(F32)).astype(BF16)
        ry_send(d, k + 4)

    def ry_end(d, part):
        t = pb[d, piece(d, y, part), :].astype(F32)
        for k in ENDS[part]:
            need(ry_wait, d, k)
            t = t + ybuf[d, k].astype(F32)
        yb[d, part] = t.astype(BF16)

    def rz_send(k):
        d = 2 if k < 2 else WAY[k] % 4
        send(yb.at[d, PART[k]], zbuf.at[k], rz_s.at[k], rz_r.at[k], h_peer[WAY[k]])

    def rz_wait(k):
        landed(zbuf.at[k], rz_s.at[k], rz_r.at[k], h_peer[WAY[k]])

    def rz_mid(k):
        need(rz_wait, k)
        d, part = WAY[k] % 4, PART[k]
        yb[d, part] = (yb[d, part].astype(F32) + zbuf[k].astype(F32)).astype(BF16)
        rz_send(k + 4)

    def rz_end(part):
        t = yb[0, part].astype(F32)
        for k in ENDS[part]:
            need(rz_wait, k)
            t = t + zbuf[k].astype(F32)
        gkv[part * half : (part + 1) * half, :] = t.astype(BF16)
        give(gkv.at[part * half : (part + 1) * half, :], gkv_hbm.at[part * half : (part + 1) * half, :])

    def gain_part(d, part):
        for k in {0: (), 1: (1, 3), 2: (4, 5), 3: (0, 2)}[d]:
            need(az_wait, k)
        p = mod4(h + d)
        t = yb[d, part].astype(F32) * blk(p, y, c, part)[...].astype(F32)
        fold = t[:, :LANES]
        for i in range(1, kvw // LANES):
            fold = fold + t[:, i * LANES : (i + 1) * LANES]
        gfold[p, pl.ds(pl.multiple_of(c * rows + part * half, half), half), :] = fold

    def gain_send():
        for p in range(4):
            gz[h, p] = jnp.sum(gfold[p].T, axis=0, keepdims=True)
        for s in (1, -1, 2):
            send(gz.at[h], gz.at[h], gg_s.at[8 + s], gg_r.at[8 + s], h_peer[s])

    def gain_pass():
        for s in (1, -1, 2):
            landed(gz.at[mod4(h - s)], gg_s.at[8 + s], gg_r.at[8 + s], h_peer[s])
        mine = y * 2 + c
        for p in range(4):
            gall[mine, p] = gz[0, p] + gz[1, p] + gz[2, p] + gz[3, p]
        for i, peer in enumerate(near):
            send(gall.at[mine], gall.at[mine], gg_s.at[i], gg_r.at[i], peer)

    def gain_end():
        for i, peer in enumerate(near_from):
            landed(gall.at[lax.rem(peer["fsdp"], 8)], gg_s.at[i], gg_r.at[i], near[i])
        for p in range(4):
            for q in range(4):
                lanes = slice((p * 4 + q) * pair, (p * 4 + q + 1) * pair)
                ggain[0:1, lanes] = (gall[2 * q, p] + gall[2 * q + 1, p]) / gain[0:1, lanes]
        give(ggain, ggain_hbm)

    def chunk(d, r):
        j = mod4(h + d) * 4 + mod4(y + r)
        lanes = pl.ds(pl.multiple_of(j * pair, pair), pair)
        ng = lax.dot_general(kv[...], wbuf[lanes, :], (((1,), (1,)), ((), ())), preferred_element_type=F32)
        unit = x[:, lanes].astype(F32) * scale[...]
        g = ng * gain[0:1, lanes]
        acc[...] += g * unit
        gb[:, lanes] = g

    def outer_first():
        loads[4].wait()
        width = feat // 4
        for i in range(4):
            dl[i] = delta[:, i * width : (i + 1) * width].astype(BF16)
        for s in (1, 2, 3):
            send(dl.at[mod4(xx + s)], dx.at[s], ox_s.at[s], ox_r.at[s], x_peer[s])

    def outer_second():
        t = dl[xx].astype(F32)
        for s in (1, 2, 3):
            landed(dx.at[s], ox_s.at[s], ox_r.at[s], x_peer[s])
            t = t + dx[s].astype(F32)
        dz[zl] = t.astype(BF16)
        for s in (1, 2, 3):
            send(dz.at[zl], dz.at[zl], og_s.at[0, s], og_r.at[0, s], l_peer[s])

    def outer_third():
        for s in (1, 2, 3):
            landed(dz.at[mod4(zl - s)], og_s.at[0, s], og_r.at[0, s], l_peer[s])
        t = dz[0].astype(F32) + dz[1].astype(F32) + dz[2].astype(F32) + dz[3].astype(F32)
        dt[xx] = t.astype(BF16)
        for s in (1, 2, 3):
            send(dt.at[xx], dt.at[xx], og_s.at[1, s], og_r.at[1, s], x_peer[s])

    def outer_last():
        for s in (1, 2, 3):
            landed(dt.at[mod4(xx - s)], og_s.at[1, s], og_r.at[1, s], x_peer[s])
        loads[5].wait()
        loads[6].wait()
        width = feat // 4
        phase = jnp.full((1, LANES), sync_ref[0].astype(F32)) / ROUNDS
        rate = (OUTER_RATE * (1.0 + jnp.cos(jnp.pi * phase)) / 2.0)[0:1, 0:1]
        for i in range(4):
            at = slice(i * width, (i + 1) * width)
            mean = dt[i].astype(F32) * (1.0 / 16)
            fresh = NESTEROV_MU * mom[:, at] + mean
            nmom[:, at] = fresh
            npar[:, at] = par[:, at] - rate * (mean + NESTEROV_MU * fresh)
        give(nmom, nmom_hbm)
        give(npar, npar_hbm)

    def az_fwd(k):
        need(az_wait, k - 4)
        az_send(k)

    def ay_first(d, part):
        need(az_wait, {(3, 0): 0, (1, 1): 1, (3, 1): 2, (1, 0): 3, (2, 0): 4, (2, 1): 5}[d, part])
        for k in ((0, 3), (1, 2))[part]:
            ay_send(d, k)

    def ay_fwd(d, k):
        need(ay_wait, d, k - 4)
        ay_send(d, k)

    def over(d, r):
        if r == 0:
            for k in {0: (), 1: (1, 3), 2: (4, 5), 3: (0, 2)}[d]:
                need(az_wait, k)
        else:
            for k in {3: (0, 2), 1: (1, 3), 2: (4, 5)}[r]:
                need(ay_wait, d, k)
        as_send(d, r)

    def mul(d, r):
        need(as_wait, d, r)
        chunk(d, r)

    acc[...] = jnp.zeros_like(acc)
    gfold[...] = jnp.zeros_like(gfold)
    kv_here = lambda: landed(kv_sib, nt_s.at[4], nt_r.at[4], sib)
    tasks = dict(
        norm=norm, kv_here=kv_here, partial=partial, az_fwd=az_fwd, ay_first=ay_first, ay_fwd=ay_fwd, over=over,
        mul=mul, ry_mid=ry_mid, ry_end=ry_end, rz_send=rz_send, rz_mid=rz_mid, rz_end=rz_end, gain_part=gain_part,
        gain_send=gain_send, gain_pass=gain_pass, gain_end=gain_end,
        outer_first=outer_first, outer_second=outer_second, outer_third=outer_third, outer_last=outer_last,
    )
    for name, *key in ORDER:
        if outer or not name.startswith("outer"):
            tasks[name](*key)
    inner = jnp.sum(acc[...], axis=-1, keepdims=True) * (1.0 / feat)
    acc[...] = jnp.broadcast_to(inner, acc.shape)

    block = min(64, tok)

    def final(i):
        at = slice(i * block, (i + 1) * block)
        sc, inn = scale[at, :], acc[at, :]
        for j in range(chunks):
            lanes = slice(j * pair, (j + 1) * pair)
            unit = x[at, lanes].astype(F32) * sc
            obuf[at, lanes] = (sc * (gb[at, lanes] - unit * inn)).astype(BF16)
        give(obuf.at[at, :], gin_hbm.at[at, :])

    for i in range(tok // block):
        final(i)
    for name, *key in LATE:
        tasks[name](*key)
    for copy in pending:
        copy.wait_send()
    for out in outs:
        out.wait()


def hand_on(*refs):
    n = 5
    ins, outs, stages, sems = refs[:n], refs[n : 2 * n], refs[2 * n : 3 * n], refs[3 * n]
    loads, stores = [], []
    for a, stage, b in zip(ins, stages, outs):
        split = 4 if a.shape[0] >= 256 else 1
        size = a.shape[0] // split
        for i in range(split):
            at = pl.ds(i * size, size)
            loads.append(pltpu.make_async_copy(a.at[at, :], stage.at[at, :], sems.at[0, len(loads)]))
            stores.append(pltpu.make_async_copy(stage.at[at, :], b.at[at, :], sems.at[1, len(stores)]))
    for load in loads:
        load.start()
    for load, store in zip(loads, stores):
        load.wait()
        store.start()
    for store in stores:
        store.wait()


def local(residual_in, norm_gain, kv_weight, kv_grad, outer_delta, outer_momentum, global_params, sync_index, outer=True):
    tok, feat = residual_in.shape[1:]
    rows, kvw = kv_weight.shape[1:]
    frag = outer_delta.shape[1]
    half, pair = rows // 2, 2 * rows
    chunks = feat // pair
    any_space = pl.BlockSpec(memory_space=pl.ANY)
    dma = pltpu.SemaphoreType.DMA
    width = feat // 4
    results = pl.pallas_call(
        functools.partial(kernel, (tok, feat, kvw, outer)),
        out_shape=(
            jax.ShapeDtypeStruct((rows, kvw), BF16),
            jax.ShapeDtypeStruct((1, feat), F32),
            jax.ShapeDtypeStruct((tok, feat), BF16),
            jax.ShapeDtypeStruct((frag, feat), F32),
            jax.ShapeDtypeStruct((frag, feat), F32),
        ),
        in_specs=[any_space] * 7 + [pl.BlockSpec(memory_space=pltpu.SMEM)],
        out_specs=(any_space,) * 5,
        scratch_shapes=[
            pltpu.VMEM((tok, feat), BF16),
            pltpu.VMEM((1, feat), F32),
            pltpu.VMEM((feat, kvw), BF16),
            pltpu.VMEM((tok, kvw), BF16),
            pltpu.VMEM((tok, kvw), BF16),
            pltpu.VMEM((2, 4, 4 * rows, tok), BF16),
            pltpu.VMEM((4, 4 * rows, tok), BF16),
            pltpu.VMEM((4, 4 * rows, kvw), BF16),
            pltpu.VMEM((4, 6, half, kvw), BF16),
            pltpu.VMEM((4, 2, half, kvw), BF16),
            pltpu.VMEM((6, half, kvw), BF16),
            pltpu.VMEM((tok, LANES), F32),
            pltpu.VMEM((tok, LANES), F32),
            pltpu.VMEM((tok, feat), F32),
            pltpu.VMEM((tok, feat), BF16),
            pltpu.VMEM((rows, kvw), BF16),
            pltpu.VMEM((1, feat), F32),
            pltpu.VMEM((frag, feat), F32),
            pltpu.VMEM((frag, feat), F32),
            pltpu.VMEM((4, pair, LANES), F32),
            pltpu.VMEM((4, 4, 1, LANES), F32),
            pltpu.VMEM((8, 4, 1, LANES), F32),
            pltpu.VMEM((frag, feat), F32),
            pltpu.VMEM((frag, feat), F32),
            pltpu.VMEM((frag, feat), F32),
            pltpu.VMEM((4, frag, width), BF16),
            pltpu.VMEM((4, frag, width), BF16),
            pltpu.VMEM((4, frag, width), BF16),
            pltpu.VMEM((4, frag, width), BF16),
            dma((7,)),
            dma((tok // min(64, tok) + 5,)),
            dma((6,)),
            dma((6,)),
            dma((4, 6)),
            dma((4, 6)),
            dma((4, 4)),
            dma((4, 4)),
            dma((5,)),
            dma((5,)),
            dma((4, 6)),
            dma((4, 6)),
            dma((6,)),
            dma((6,)),
            dma((4,)),
            dma((4,)),
            dma((2, 4)),
            dma((2, 4)),
            dma((11,)),
            dma((11,)),
        ],
        compiler_params=pltpu.CompilerParams(
            collective_id=0, has_side_effects=True, vmem_limit_bytes=56 * 1024 * 1024
        ),
    )(
        residual_in[0],
        norm_gain,
        kv_weight[0],
        kv_grad[0],
        outer_delta[0],
        outer_momentum,
        global_params,
        sync_index,
    )
    grad_kv, grad_gain, grad_input, new_params, new_momentum = pl.pallas_call(
        hand_on,
        out_shape=tuple(jax.ShapeDtypeStruct(r.shape, r.dtype) for r in results),
        in_specs=[any_space] * 5,
        out_specs=(any_space,) * 5,
        scratch_shapes=[pltpu.VMEM(r.shape, r.dtype) for r in results] + [dma((2, 8))],
        compiler_params=pltpu.CompilerParams(vmem_limit_bytes=60 * 1024 * 1024),
    )(*results)
    return (grad_kv[None], grad_gain, grad_input[None], new_params, new_momentum)


def solution(mesh):
    placed = (
        P("rep", "fsdp", None),
        P("rep", None),
        P("rep", "fsdp", None),
        P("rep", "fsdp", None),
        P("rep", "fsdp", None),
        P("fsdp", None),
        P("fsdp", None),
        P(),
    )
    return jax.shard_map(
        local,
        mesh=mesh,
        in_specs=placed,
        out_specs=(
            P("rep", "fsdp", None),
            P("rep", None),
            P("rep", "fsdp", None),
            P("fsdp", None),
            P("fsdp", None),
        ),
        check_vma=False,
    )
```

```python
import functools

import jax
import jax.numpy as jnp
from jax import lax
from jax.experimental import pallas as pl
from jax.experimental.pallas import tpu as pltpu
from jax.sharding import PartitionSpec as P

ROUNDS = 64
EPSILON = 1e-05
NESTEROV_MU = 0.9
OUTER_RATE = 0.7
MESH = pl.DeviceIdType.MESH
F32, BF16 = jnp.float32, jnp.bfloat16
LANES = 128


ORDER = (
    ("norm", 2),
    ("norm", 1),
    ("norm", 3),
    ("norm", 0),
    ("mul", 0, 0),
    ("ay_fwd", 0, 4),
    ("ay_fwd", 0, 5),
    ("over", 0, 1),
    ("over", 0, 3),
    ("kv_here",),
    ("partial", 2),
    ("outer_first",),
    ("partial", 1),
    ("over", 0, 2),
    ("partial", 3),
    ("partial", 0),
    ("outer_second",),
    ("mul", 0, 1),
    ("mul", 0, 2),
    ("mul", 0, 3),
    ("az_fwd", 4),
    ("az_fwd", 5),
    ("over", 1, 0),
    ("over", 3, 0),
    ("ry_mid", 2, 0),
    ("ry_mid", 2, 1),
    ("ay_first", 1, 1),
    ("ay_first", 1, 0),
    ("ay_first", 3, 0),
    ("ay_first", 3, 1),
    ("outer_third",),
    ("mul", 1, 0),
    ("mul", 3, 0),
    ("outer_last",),
    ("ry_mid", 1, 1),
    ("ry_mid", 1, 0),
    ("ay_first", 2, 0),
    ("ay_first", 2, 1),
    ("over", 2, 0),
    ("mul", 2, 0),
    ("ry_mid", 3, 0),
    ("ry_mid", 3, 1),
    ("ry_mid", 0, 1),
    ("ry_mid", 0, 0),
    ("ry_end", 2, 0),
    ("rz_send", 0),
    ("ry_end", 2, 1),
    ("rz_send", 1),
    ("ay_fwd", 1, 4),
    ("ay_fwd", 1, 5),
    ("ay_fwd", 3, 4),
    ("ay_fwd", 3, 5),
    ("over", 1, 1),
    ("over", 1, 3),
    ("over", 3, 1),
    ("over", 3, 3),
    ("gain_part", 2, 0),
    ("gain_part", 2, 1),
    ("mul", 1, 1),
    ("mul", 1, 3),
    ("mul", 3, 1),
    ("mul", 3, 3),
    ("ry_end", 1, 1),
    ("rz_send", 2),
    ("ry_end", 1, 0),
    ("gain_part", 1, 0),
    ("ay_fwd", 2, 4),
    ("ay_fwd", 2, 5),
    ("over", 2, 1),
    ("over", 2, 3),
    ("gain_part", 1, 1),
    ("ry_end", 3, 0),
    ("rz_send", 3),
    ("ry_end", 3, 1),
    ("gain_part", 3, 0),
    ("gain_part", 3, 1),
    ("ry_end", 0, 0),
    ("ry_end", 0, 1),
    ("gain_part", 0, 0),
    ("gain_part", 0, 1),
    ("gain_send",),
    ("mul", 2, 1),
    ("mul", 2, 3),
    ("over", 1, 2),
    ("over", 3, 2),
    ("over", 2, 2),
    ("rz_mid", 1),
    ("mul", 1, 2),
    ("mul", 3, 2),
    ("rz_mid", 0),
    ("mul", 2, 2),
)
LATE = (
    ("gain_pass",),
    ("gain_end",),
    ("rz_end", 0),
    ("rz_end", 1),
)


def kernel(
    sizes,
    resid_hbm,
    gain_hbm,
    w_hbm,
    kv_hbm,
    delta_hbm,
    mom_hbm,
    par_hbm,
    sync_ref,
    gkv,
    ggain,
    obuf,
    npar,
    nmom,
    x,
    gain,
    wbuf,
    kv,
    kv_sib,
    nt,
    nt_sib,
    pb,
    ybuf,
    yb,
    zbuf,
    scale,
    acc,
    gb,
    gfold,
    gz,
    gall,
    delta,
    mom,
    par,
    dl,
    dx,
    dz,
    dt,
    sem_in,
    az_s,
    az_r,
    ay_s,
    ay_r,
    as_s,
    as_r,
    nt_s,
    nt_r,
    ry_s,
    ry_r,
    rz_s,
    rz_r,
    ox_s,
    ox_r,
    og_s,
    og_r,
    gg_s,
    gg_r,
):
    tok, feat, kvw, outer = sizes
    rows = w_hbm.shape[0]
    half = rows // 2
    pair = 2 * rows
    chunks = feat // pair
    f = lax.axis_index("fsdp")
    c = lax.rem(f, 2)
    y = lax.rem(lax.div(f, 2), 4)
    h = lax.div(f, 8)
    rep = lax.axis_index("rep")
    xx = lax.rem(rep, 4)
    zl = lax.div(rep, 4)

    def mod4(v):
        return lax.rem(v + 8, 4)

    def inside(hh, yy, cc):
        return {"fsdp": (hh * 4 + yy) * 2 + cc}

    sib = inside(h, y, 1 - c)
    y_peer = {s: inside(h, mod4(y + s), c) for s in (1, -1, 2)}
    h_peer = {s: inside(mod4(h + s), y, c) for s in (1, -1, 2)}
    x_peer = {s: {"rep": zl * 4 + mod4(xx + s)} for s in (1, 2, 3)}
    l_peer = {s: {"rep": mod4(zl + s) * 4 + xx} for s in (1, 2, 3)}

    barrier = pltpu.get_barrier_semaphore()
    near = [sib] + [inside(h, mod4(y + s), cc) for s in (1, -1, 2) for cc in (c, 1 - c)]
    near_from = near[:1] + [inside(h, mod4(y - s), cc) for s in (1, -1, 2) for cc in (c, 1 - c)]
    peers = near + list(h_peer.values())
    if outer:
        peers += list(x_peer.values()) + list(l_peer.values())
    for peer in peers:
        pl.semaphore_signal(barrier, inc=1, device_id=peer, device_id_type=MESH)

    def blk(p, yy, cc, part=None):
        start = ((p * 4 + yy) * 2 + cc) * rows
        if part is None:
            return wbuf.at[pl.ds(pl.multiple_of(start, rows), rows), :]
        return wbuf.at[pl.ds(pl.multiple_of(start + part * half, half), half), :]

    own_copies = [
        (resid_hbm, x),
        (kv_hbm, kv),
        (gain_hbm, gain),
        (w_hbm, blk(h, y, c)),
        (delta_hbm, delta),
        (mom_hbm, mom),
        (par_hbm, par),
    ]
    loads = [pltpu.make_async_copy(a, b, sem_in.at[i]) for i, (a, b) in enumerate(own_copies)]
    for i in (3, 1, 0, 2, 4, 5, 6):
        loads[i].start()

    pending = []

    def send(src, dst, ssem, rsem, peer):
        copy = pltpu.make_async_remote_copy(
            src_ref=src, dst_ref=dst, send_sem=ssem, recv_sem=rsem, device_id=peer, device_id_type=MESH
        )
        copy.start()
        pending.append(copy)

    def landed(dst, ssem, rsem, peer):
        pltpu.make_async_remote_copy(
            src_ref=dst, dst_ref=dst, send_sem=ssem, recv_sem=rsem, device_id=peer, device_id_type=MESH
        ).wait_recv()

    loads[3].wait()
    pl.semaphore_wait(barrier, len(peers))

    seen = set()

    def need(wait, *key):
        if (wait, key) not in seen:
            seen.add((wait, key))
            wait(*key)

    PART = (0, 1, 1, 0, 0, 1)
    WAY = (1, -1, 1, -1, 1, -1)

    def az_send(k):
        if k < 4:
            src = dst = blk(h, y, c, PART[k])
        else:
            src = dst = blk(mod4(h - WAY[k]), y, c, PART[k])
        send(src, dst, az_s.at[k], az_r.at[k], h_peer[WAY[k]])

    def az_wait(k):
        p = mod4(h - WAY[k] * (1 if k < 4 else 2))
        landed(blk(p, y, c, PART[k]), az_s.at[k], az_r.at[k], h_peer[WAY[k]])

    def ay_send(d, k):
        p = mod4(h + d)
        if k < 4:
            src = dst = blk(p, y, c, PART[k])
        else:
            src = dst = blk(p, mod4(y - WAY[k]), c, PART[k])
        send(src, dst, ay_s.at[d, k], ay_r.at[d, k], y_peer[WAY[k]])

    def ay_wait(d, k):
        yy = mod4(y - WAY[k] * (1 if k < 4 else 2))
        landed(blk(mod4(h + d), yy, c, PART[k]), ay_s.at[d, k], ay_r.at[d, k], y_peer[WAY[k]])

    def as_send(d, r):
        b = blk(mod4(h + d), mod4(y + r), c)
        send(b, b, as_s.at[d, r], as_r.at[d, r], sib)

    def as_wait(d, r):
        landed(blk(mod4(h + d), mod4(y + r), 1 - c), as_s.at[d, r], as_r.at[d, r], sib)

    for k in (0, 1, 2, 3):
        az_send(k)
    for k in (0, 1, 2, 3):
        ay_send(0, k)
    loads[1].wait()
    send(kv, kv_sib, nt_s.at[4], nt_r.at[4], sib)
    as_send(0, 0)

    loads[0].wait()
    loads[2].wait()

    @pl.loop(0, tok // 32)
    def _(i):
        at = pl.ds(pl.multiple_of(i * 32, 32), 32)
        v = x[at, :].astype(F32)
        mean = jnp.mean(v * v, axis=-1, keepdims=True)
        scale[at, :] = jnp.broadcast_to(lax.rsqrt(mean + EPSILON), (32, LANES))

    def norm(d):
        p = mod4(h + d)

        @pl.loop(0, 4)
        def _(yy):
            lanes = pl.ds(pl.multiple_of((p * 4 + yy) * pair, pair), pair)
            unit = x[:, lanes].astype(F32) * scale[...]
            t = (unit * gain[0:1, lanes]).astype(BF16).T
            at = pl.ds(pl.multiple_of(yy * rows, rows), rows)
            nt[0, d, at, :] = t[:rows]
            nt[1, d, at, :] = t[rows:]

        send(nt.at[1 - c, d], nt_sib.at[d], nt_s.at[d], nt_r.at[d], sib)

    def partial(d):
        landed(nt_sib.at[d], nt_s.at[d], nt_r.at[d], sib)
        step = min(256, kvw)

        @pl.loop(0, kvw // step)
        def _(i):
            at = pl.ds(pl.multiple_of(i * step, step), step)
            t = jnp.dot(nt[c, d], kv[:, at], preferred_element_type=F32)
            t = t + jnp.dot(nt_sib[d], kv_sib[:, at], preferred_element_type=F32)
            pb[d, :, at] = t.astype(BF16)

        for k in (0, 1, 2, 3):
            ry_send(d, k)

    def piece(d, yy, part):
        return pl.ds(pl.multiple_of(mod4(yy) * rows + part * half, half), half)

    def ry_send(d, k):
        dest = y + (2 * WAY[k] if k < 2 else WAY[k])
        send(pb.at[d, piece(d, dest, PART[k]), :], ybuf.at[d, k], ry_s.at[d, k], ry_r.at[d, k], y_peer[WAY[k]])

    def ry_wait(d, k):
        landed(ybuf.at[d, k], ry_s.at[d, k], ry_r.at[d, k], y_peer[WAY[k]])

    ENDS = ((3, 4), (2, 5))

    def ry_mid(d, k):
        need(ry_wait, d, k)
        at = piece(d, y + WAY[k], PART[k])
        pb[d, at, :] = (pb[d, at, :].astype(F32) + ybuf[d, k].astype(F32)).astype(BF16)
        ry_send(d, k + 4)

    def ry_end(d, part):
        t = pb[d, piece(d, y, part), :].astype(F32)
        for k in ENDS[part]:
            need(ry_wait, d, k)
            t = t + ybuf[d, k].astype(F32)
        yb[d, part] = t.astype(BF16)

    def rz_send(k):
        d = 2 if k < 2 else WAY[k] % 4
        send(yb.at[d, PART[k]], zbuf.at[k], rz_s.at[k], rz_r.at[k], h_peer[WAY[k]])

    def rz_wait(k):
        landed(zbuf.at[k], rz_s.at[k], rz_r.at[k], h_peer[WAY[k]])

    def rz_mid(k):
        need(rz_wait, k)
        d, part = WAY[k] % 4, PART[k]
        yb[d, part] = (yb[d, part].astype(F32) + zbuf[k].astype(F32)).astype(BF16)
        rz_send(k + 4)

    def rz_end(part):
        t = yb[0, part].astype(F32)
        for k in ENDS[part]:
            need(rz_wait, k)
            t = t + zbuf[k].astype(F32)
        gkv[part * half : (part + 1) * half, :] = t.astype(BF16)

    def gain_part(d, part):
        for k in {0: (), 1: (1, 3), 2: (4, 5), 3: (0, 2)}[d]:
            need(az_wait, k)
        p = mod4(h + d)
        t = yb[d, part].astype(F32) * blk(p, y, c, part)[...].astype(F32)
        fold = t[:, :LANES]
        for i in range(1, kvw // LANES):
            fold = fold + t[:, i * LANES : (i + 1) * LANES]
        gfold[p, pl.ds(pl.multiple_of(c * rows + part * half, half), half), :] = fold

    def gain_send():
        for p in range(4):
            gz[h, p] = jnp.sum(gfold[p].T, axis=0, keepdims=True)
        for s in (1, -1, 2):
            send(gz.at[h], gz.at[h], gg_s.at[8 + s], gg_r.at[8 + s], h_peer[s])

    def gain_pass():
        for s in (1, -1, 2):
            landed(gz.at[mod4(h - s)], gg_s.at[8 + s], gg_r.at[8 + s], h_peer[s])
        mine = y * 2 + c
        for p in range(4):
            gall[mine, p] = gz[0, p] + gz[1, p] + gz[2, p] + gz[3, p]
        for i, peer in enumerate(near):
            send(gall.at[mine], gall.at[mine], gg_s.at[i], gg_r.at[i], peer)

    def gain_end():
        for i, peer in enumerate(near_from):
            landed(gall.at[lax.rem(peer["fsdp"], 8)], gg_s.at[i], gg_r.at[i], near[i])
        for p in range(4):
            for q in range(4):
                lanes = slice((p * 4 + q) * pair, (p * 4 + q + 1) * pair)
                ggain[0:1, lanes] = (gall[2 * q, p] + gall[2 * q + 1, p]) / gain[0:1, lanes]

    def chunk(d, r):
        j = mod4(h + d) * 4 + mod4(y + r)
        lanes = pl.ds(pl.multiple_of(j * pair, pair), pair)
        ng = lax.dot_general(kv[...], wbuf[lanes, :], (((1,), (1,)), ((), ())), preferred_element_type=F32)
        unit = x[:, lanes].astype(F32) * scale[...]
        g = ng * gain[0:1, lanes]
        acc[...] += g * unit
        gb[:, lanes] = g

    def outer_first():
        loads[4].wait()
        width = feat // 4
        for i in range(4):
            dl[i] = delta[:, i * width : (i + 1) * width].astype(BF16)
        for s in (1, 2, 3):
            send(dl.at[mod4(xx + s)], dx.at[s], ox_s.at[s], ox_r.at[s], x_peer[s])

    def outer_second():
        t = dl[xx].astype(F32)
        for s in (1, 2, 3):
            landed(dx.at[s], ox_s.at[s], ox_r.at[s], x_peer[s])
            t = t + dx[s].astype(F32)
        dz[zl] = t.astype(BF16)
        for s in (1, 2, 3):
            send(dz.at[zl], dz.at[zl], og_s.at[0, s], og_r.at[0, s], l_peer[s])

    def outer_third():
        for s in (1, 2, 3):
            landed(dz.at[mod4(zl - s)], og_s.at[0, s], og_r.at[0, s], l_peer[s])
        t = dz[0].astype(F32) + dz[1].astype(F32) + dz[2].astype(F32) + dz[3].astype(F32)
        dt[xx] = t.astype(BF16)
        for s in (1, 2, 3):
            send(dt.at[xx], dt.at[xx], og_s.at[1, s], og_r.at[1, s], x_peer[s])

    def outer_last():
        for s in (1, 2, 3):
            landed(dt.at[mod4(xx - s)], og_s.at[1, s], og_r.at[1, s], x_peer[s])
        loads[5].wait()
        loads[6].wait()
        width = feat // 4
        phase = jnp.full((1, LANES), sync_ref[0].astype(F32)) / ROUNDS
        rate = (OUTER_RATE * (1.0 + jnp.cos(jnp.pi * phase)) / 2.0)[0:1, 0:1]
        for i in range(4):
            at = slice(i * width, (i + 1) * width)
            mean = dt[i].astype(F32) * (1.0 / 16)
            fresh = NESTEROV_MU * mom[:, at] + mean
            nmom[:, at] = fresh
            npar[:, at] = par[:, at] - rate * (mean + NESTEROV_MU * fresh)

    def az_fwd(k):
        need(az_wait, k - 4)
        az_send(k)

    def ay_first(d, part):
        need(az_wait, {(3, 0): 0, (1, 1): 1, (3, 1): 2, (1, 0): 3, (2, 0): 4, (2, 1): 5}[d, part])
        for k in ((0, 3), (1, 2))[part]:
            ay_send(d, k)

    def ay_fwd(d, k):
        need(ay_wait, d, k - 4)
        ay_send(d, k)

    def over(d, r):
        if r == 0:
            for k in {0: (), 1: (1, 3), 2: (4, 5), 3: (0, 2)}[d]:
                need(az_wait, k)
        else:
            for k in {3: (0, 2), 1: (1, 3), 2: (4, 5)}[r]:
                need(ay_wait, d, k)
        as_send(d, r)

    def mul(d, r):
        need(as_wait, d, r)
        chunk(d, r)

    acc[...] = jnp.zeros_like(acc)
    gfold[...] = jnp.zeros_like(gfold)
    kv_here = lambda: landed(kv_sib, nt_s.at[4], nt_r.at[4], sib)
    tasks = dict(
        norm=norm, kv_here=kv_here, partial=partial, az_fwd=az_fwd, ay_first=ay_first, ay_fwd=ay_fwd, over=over,
        mul=mul, ry_mid=ry_mid, ry_end=ry_end, rz_send=rz_send, rz_mid=rz_mid, rz_end=rz_end, gain_part=gain_part,
        gain_send=gain_send, gain_pass=gain_pass, gain_end=gain_end,
        outer_first=outer_first, outer_second=outer_second, outer_third=outer_third, outer_last=outer_last,
    )
    for name, *key in ORDER:
        if outer or not name.startswith("outer"):
            tasks[name](*key)
    inner = jnp.sum(acc[...], axis=-1, keepdims=True) * (1.0 / feat)
    acc[...] = jnp.broadcast_to(inner, acc.shape)

    block = min(64, tok)

    def final(i):
        at = slice(i * block, (i + 1) * block)
        sc, inn = scale[at, :], acc[at, :]
        for j in range(chunks):
            lanes = slice(j * pair, (j + 1) * pair)
            unit = x[at, lanes].astype(F32) * sc
            obuf[at, lanes] = (sc * (gb[at, lanes] - unit * inn)).astype(BF16)

    for i in range(tok // block):
        final(i)
    for name, *key in LATE:
        tasks[name](*key)
    for copy in pending:
        copy.wait_send()


def hand_on(*refs):
    n = len(refs) // 2
    ins, outs, sems = refs[:n], refs[n : 2 * n], refs[2 * n]
    copies = []
    for a, b in zip(ins, outs):
        split = 4 if a.shape[0] >= 256 else 1
        size = a.shape[0] // split
        for i in range(split):
            at = pl.ds(i * size, size)
            copies.append(pltpu.make_async_copy(a.at[at, :], b.at[at, :], sems.at[len(copies)]))
    for copy in copies:
        copy.start()
    for copy in copies:
        copy.wait()


def local(residual_in, norm_gain, kv_weight, kv_grad, outer_delta, outer_momentum, global_params, sync_index, outer=True):
    tok, feat = residual_in.shape[1:]
    rows, kvw = kv_weight.shape[1:]
    frag = outer_delta.shape[1]
    half, pair = rows // 2, 2 * rows
    chunks = feat // pair
    any_space = pl.BlockSpec(memory_space=pl.ANY)
    dma = pltpu.SemaphoreType.DMA
    width = feat // 4
    results = pl.pallas_call(
        functools.partial(kernel, (tok, feat, kvw, outer)),
        out_shape=(
            pltpu.VMEM((rows, kvw), BF16),
            pltpu.VMEM((1, feat), F32),
            pltpu.VMEM((tok, feat), BF16),
            pltpu.VMEM((frag, feat), F32),
            pltpu.VMEM((frag, feat), F32),
        ),
        in_specs=[any_space] * 7 + [pl.BlockSpec(memory_space=pltpu.SMEM)],
        out_specs=(pl.BlockSpec(memory_space=pltpu.VMEM),) * 5,
        scratch_shapes=[
            pltpu.VMEM((tok, feat), BF16),
            pltpu.VMEM((1, feat), F32),
            pltpu.VMEM((feat, kvw), BF16),
            pltpu.VMEM((tok, kvw), BF16),
            pltpu.VMEM((tok, kvw), BF16),
            pltpu.VMEM((2, 4, 4 * rows, tok), BF16),
            pltpu.VMEM((4, 4 * rows, tok), BF16),
            pltpu.VMEM((4, 4 * rows, kvw), BF16),
            pltpu.VMEM((4, 6, half, kvw), BF16),
            pltpu.VMEM((4, 2, half, kvw), BF16),
            pltpu.VMEM((6, half, kvw), BF16),
            pltpu.VMEM((tok, LANES), F32),
            pltpu.VMEM((tok, LANES), F32),
            pltpu.VMEM((tok, feat), F32),
            pltpu.VMEM((4, pair, LANES), F32),
            pltpu.VMEM((4, 4, 1, LANES), F32),
            pltpu.VMEM((8, 4, 1, LANES), F32),
            pltpu.VMEM((frag, feat), F32),
            pltpu.VMEM((frag, feat), F32),
            pltpu.VMEM((frag, feat), F32),
            pltpu.VMEM((4, frag, width), BF16),
            pltpu.VMEM((4, frag, width), BF16),
            pltpu.VMEM((4, frag, width), BF16),
            pltpu.VMEM((4, frag, width), BF16),
            dma((7,)),
            dma((6,)),
            dma((6,)),
            dma((4, 6)),
            dma((4, 6)),
            dma((4, 4)),
            dma((4, 4)),
            dma((5,)),
            dma((5,)),
            dma((4, 6)),
            dma((4, 6)),
            dma((6,)),
            dma((6,)),
            dma((4,)),
            dma((4,)),
            dma((2, 4)),
            dma((2, 4)),
            dma((11,)),
            dma((11,)),
        ],
        compiler_params=pltpu.CompilerParams(
            collective_id=0, has_side_effects=True, vmem_limit_bytes=60 * 1024 * 1024
        ),
    )(
        residual_in[0],
        norm_gain,
        kv_weight[0],
        kv_grad[0],
        outer_delta[0],
        outer_momentum,
        global_params,
        sync_index,
    )
    grad_kv, grad_gain, grad_input, new_params, new_momentum = pl.pallas_call(
        hand_on,
        out_shape=tuple(jax.ShapeDtypeStruct(r.shape, r.dtype) for r in results),
        in_specs=[pl.BlockSpec(memory_space=pltpu.VMEM)] * 5,
        out_specs=(any_space,) * 5,
        scratch_shapes=[dma((8,))],
        compiler_params=pltpu.CompilerParams(vmem_limit_bytes=8 * 1024 * 1024),
    )(*results)
    return (grad_kv[None], grad_gain, grad_input[None], new_params, new_momentum)


def solution(mesh):
    placed = (
        P("rep", "fsdp", None),
        P("rep", None),
        P("rep", "fsdp", None),
        P("rep", "fsdp", None),
        P("rep", "fsdp", None),
        P("fsdp", None),
        P("fsdp", None),
        P(),
    )
    return jax.shard_map(
        local,
        mesh=mesh,
        in_specs=placed,
        out_specs=(
            P("rep", "fsdp", None),
            P("rep", None),
            P("rep", "fsdp", None),
            P("fsdp", None),
            P("fsdp", None),
        ),
        check_vma=False,
    )
```

```python
import functools

import jax
import jax.numpy as jnp
from jax import lax
from jax.experimental import pallas as pl
from jax.experimental.pallas import tpu as pltpu
from jax.sharding import PartitionSpec as P

ROUNDS = 64
EPSILON = 1e-05
NESTEROV_MU = 0.9
OUTER_RATE = 0.7
MESH = pl.DeviceIdType.MESH
F32, BF16 = jnp.float32, jnp.bfloat16
LANES = 128


ORDER = (
    ("norm", 2),
    ("norm", 1),
    ("norm", 3),
    ("norm", 0),
    ("mul", 0, 0),
    ("ay_fwd", 0, 4),
    ("ay_fwd", 0, 5),
    ("over", 0, 1),
    ("over", 0, 3),
    ("kv_here",),
    ("partial", 2),
    ("outer_first",),
    ("partial", 1),
    ("over", 0, 2),
    ("partial", 3),
    ("partial", 0),
    ("outer_second",),
    ("mul", 0, 1),
    ("mul", 0, 2),
    ("mul", 0, 3),
    ("az_fwd", 4),
    ("az_fwd", 5),
    ("over", 1, 0),
    ("over", 3, 0),
    ("ry_mid", 2, 0),
    ("ry_mid", 2, 1),
    ("ay_first", 1, 1),
    ("ay_first", 1, 0),
    ("ay_first", 3, 0),
    ("ay_first", 3, 1),
    ("mul", 1, 0),
    ("mul", 3, 0),
    ("ry_mid", 1, 1),
    ("ry_mid", 1, 0),
    ("ay_first", 2, 0),
    ("ay_first", 2, 1),
    ("over", 2, 0),
    ("mul", 2, 0),
    ("ry_mid", 3, 0),
    ("ry_mid", 3, 1),
    ("ry_mid", 0, 1),
    ("ry_mid", 0, 0),
    ("outer_third",),
    ("ry_end", 2, 0),
    ("rz_send", 0),
    ("ry_end", 2, 1),
    ("rz_send", 1),
    ("ay_fwd", 1, 4),
    ("ay_fwd", 1, 5),
    ("ay_fwd", 3, 4),
    ("ay_fwd", 3, 5),
    ("over", 1, 1),
    ("over", 1, 3),
    ("over", 3, 1),
    ("over", 3, 3),
    ("gain_part", 2, 0),
    ("gain_part", 2, 1),
    ("mul", 1, 1),
    ("mul", 1, 3),
    ("mul", 3, 1),
    ("mul", 3, 3),
    ("ry_end", 1, 1),
    ("rz_send", 2),
    ("ry_end", 1, 0),
    ("gain_part", 1, 0),
    ("ay_fwd", 2, 4),
    ("ay_fwd", 2, 5),
    ("over", 2, 1),
    ("over", 2, 3),
    ("gain_part", 1, 1),
    ("ry_end", 3, 0),
    ("rz_send", 3),
    ("ry_end", 3, 1),
    ("gain_part", 3, 0),
    ("gain_part", 3, 1),
    ("ry_end", 0, 0),
    ("ry_end", 0, 1),
    ("gain_part", 0, 0),
    ("gain_part", 0, 1),
    ("gain_send",),
    ("outer_last",),
    ("mul", 2, 1),
    ("mul", 2, 3),
    ("over", 1, 2),
    ("over", 3, 2),
    ("over", 2, 2),
    ("rz_mid", 1),
    ("mul", 1, 2),
    ("mul", 3, 2),
    ("rz_mid", 0),
    ("mul", 2, 2),
)
LATE = (
    ("gain_pass",),
    ("rz_end", 0),
    ("rz_end", 1),
    ("gain_end",),
)


def kernel(
    sizes,
    resid_hbm,
    gain_hbm,
    w_hbm,
    kv_hbm,
    delta_hbm,
    mom_hbm,
    par_hbm,
    sync_ref,
    gkv,
    ggain,
    obuf,
    npar,
    nmom,
    x,
    gain,
    wbuf,
    kv,
    kv_sib,
    nt,
    nt_sib,
    pb,
    ybuf,
    yb,
    zbuf,
    scale,
    acc,
    gb,
    gfold,
    gz,
    gall,
    delta,
    mom,
    par,
    dl,
    dx,
    dz,
    dt,
    sem_in,
    az_s,
    az_r,
    ay_s,
    ay_r,
    as_s,
    as_r,
    nt_s,
    nt_r,
    ry_s,
    ry_r,
    rz_s,
    rz_r,
    ox_s,
    ox_r,
    og_s,
    og_r,
    gg_s,
    gg_r,
):
    tok, feat, kvw, outer = sizes
    rows = w_hbm.shape[0]
    half = rows // 2
    pair = 2 * rows
    chunks = feat // pair
    f = lax.axis_index("fsdp")
    c = lax.rem(f, 2)
    y = lax.rem(lax.div(f, 2), 4)
    h = lax.div(f, 8)
    rep = lax.axis_index("rep")
    xx = lax.rem(rep, 4)
    zl = lax.div(rep, 4)

    def mod4(v):
        return lax.rem(v + 8, 4)

    def inside(hh, yy, cc):
        return {"fsdp": (hh * 4 + yy) * 2 + cc}

    sib = inside(h, y, 1 - c)
    y_peer = {s: inside(h, mod4(y + s), c) for s in (1, -1, 2)}
    h_peer = {s: inside(mod4(h + s), y, c) for s in (1, -1, 2)}
    x_peer = {s: {"rep": zl * 4 + mod4(xx + s)} for s in (1, 2, 3)}
    l_peer = {s: {"rep": mod4(zl + s) * 4 + xx} for s in (1, 2, 3)}

    barrier = pltpu.get_barrier_semaphore()
    near = [sib] + [inside(h, mod4(y + s), cc) for s in (1, -1, 2) for cc in (c, 1 - c)]
    near_from = near[:1] + [inside(h, mod4(y - s), cc) for s in (1, -1, 2) for cc in (c, 1 - c)]
    peers = list(h_peer.values())
    if outer:
        peers += list(l_peer.values()) + list(x_peer.values())
    peers += near
    for peer in peers:
        pl.semaphore_signal(barrier, inc=1, device_id=peer, device_id_type=MESH)

    def blk(p, yy, cc, part=None):
        start = ((p * 4 + yy) * 2 + cc) * rows
        if part is None:
            return wbuf.at[pl.ds(pl.multiple_of(start, rows), rows), :]
        return wbuf.at[pl.ds(pl.multiple_of(start + part * half, half), half), :]

    own_copies = [
        (resid_hbm, x),
        (kv_hbm, kv),
        (gain_hbm, gain),
        (w_hbm, blk(h, y, c)),
        (delta_hbm, delta),
        (mom_hbm, mom),
        (par_hbm, par),
    ]
    loads = [pltpu.make_async_copy(a, b, sem_in.at[i]) for i, (a, b) in enumerate(own_copies)]
    for i in (3, 1, 0, 2, 4, 5, 6):
        loads[i].start()

    pending = []

    def send(src, dst, ssem, rsem, peer):
        copy = pltpu.make_async_remote_copy(
            src_ref=src, dst_ref=dst, send_sem=ssem, recv_sem=rsem, device_id=peer, device_id_type=MESH
        )
        copy.start()
        pending.append(copy)

    def landed(dst, ssem, rsem, peer):
        pltpu.make_async_remote_copy(
            src_ref=dst, dst_ref=dst, send_sem=ssem, recv_sem=rsem, device_id=peer, device_id_type=MESH
        ).wait_recv()

    loads[3].wait()
    pl.semaphore_wait(barrier, len(peers))

    seen = set()

    def need(wait, *key):
        if (wait, key) not in seen:
            seen.add((wait, key))
            wait(*key)

    PART = (0, 1, 1, 0, 0, 1)
    WAY = (1, -1, 1, -1, 1, -1)

    def az_send(k):
        if k < 4:
            src = dst = blk(h, y, c, PART[k])
        else:
            src = dst = blk(mod4(h - WAY[k]), y, c, PART[k])
        send(src, dst, az_s.at[k], az_r.at[k], h_peer[WAY[k]])

    def az_wait(k):
        p = mod4(h - WAY[k] * (1 if k < 4 else 2))
        landed(blk(p, y, c, PART[k]), az_s.at[k], az_r.at[k], h_peer[WAY[k]])

    def ay_send(d, k):
        p = mod4(h + d)
        if k < 4:
            src = dst = blk(p, y, c, PART[k])
        else:
            src = dst = blk(p, mod4(y - WAY[k]), c, PART[k])
        send(src, dst, ay_s.at[d, k], ay_r.at[d, k], y_peer[WAY[k]])

    def ay_wait(d, k):
        yy = mod4(y - WAY[k] * (1 if k < 4 else 2))
        landed(blk(mod4(h + d), yy, c, PART[k]), ay_s.at[d, k], ay_r.at[d, k], y_peer[WAY[k]])

    def as_send(d, r):
        b = blk(mod4(h + d), mod4(y + r), c)
        send(b, b, as_s.at[d, r], as_r.at[d, r], sib)

    def as_wait(d, r):
        landed(blk(mod4(h + d), mod4(y + r), 1 - c), as_s.at[d, r], as_r.at[d, r], sib)

    for k in (0, 1, 2, 3):
        az_send(k)
    for k in (0, 1, 2, 3):
        ay_send(0, k)
    loads[1].wait()
    send(kv, kv_sib, nt_s.at[4], nt_r.at[4], sib)
    as_send(0, 0)

    loads[0].wait()
    loads[2].wait()

    @pl.loop(0, tok // 32)
    def _(i):
        at = pl.ds(pl.multiple_of(i * 32, 32), 32)
        v = x[at, :].astype(F32)
        mean = jnp.mean(v * v, axis=-1, keepdims=True)
        scale[at, :] = jnp.broadcast_to(lax.rsqrt(mean + EPSILON), (32, LANES))

    def norm(d):
        p = mod4(h + d)

        @pl.loop(0, 4)
        def _(yy):
            lanes = pl.ds(pl.multiple_of((p * 4 + yy) * pair, pair), pair)
            unit = x[:, lanes].astype(F32) * scale[...]
            t = (unit * gain[0:1, lanes]).astype(BF16).T
            at = pl.ds(pl.multiple_of(yy * rows, rows), rows)
            nt[0, d, at, :] = t[:rows]
            nt[1, d, at, :] = t[rows:]

        send(nt.at[1 - c, d], nt_sib.at[d], nt_s.at[d], nt_r.at[d], sib)

    def partial(d):
        landed(nt_sib.at[d], nt_s.at[d], nt_r.at[d], sib)
        step = min(256, kvw)

        @pl.loop(0, kvw // step)
        def _(i):
            at = pl.ds(pl.multiple_of(i * step, step), step)
            t = jnp.dot(nt[c, d], kv[:, at], preferred_element_type=F32)
            t = t + jnp.dot(nt_sib[d], kv_sib[:, at], preferred_element_type=F32)
            pb[d, :, at] = t.astype(BF16)

        for k in (0, 1, 2, 3):
            ry_send(d, k)

    def piece(d, yy, part):
        return pl.ds(pl.multiple_of(mod4(yy) * rows + part * half, half), half)

    def ry_send(d, k):
        dest = y + (2 * WAY[k] if k < 2 else WAY[k])
        send(pb.at[d, piece(d, dest, PART[k]), :], ybuf.at[d, k], ry_s.at[d, k], ry_r.at[d, k], y_peer[WAY[k]])

    def ry_wait(d, k):
        landed(ybuf.at[d, k], ry_s.at[d, k], ry_r.at[d, k], y_peer[WAY[k]])

    ENDS = ((3, 4), (2, 5))

    def ry_mid(d, k):
        need(ry_wait, d, k)
        at = piece(d, y + WAY[k], PART[k])
        pb[d, at, :] = (pb[d, at, :].astype(F32) + ybuf[d, k].astype(F32)).astype(BF16)
        ry_send(d, k + 4)

    def ry_end(d, part):
        t = pb[d, piece(d, y, part), :].astype(F32)
        for k in ENDS[part]:
            need(ry_wait, d, k)
            t = t + ybuf[d, k].astype(F32)
        yb[d, part] = t.astype(BF16)

    def rz_send(k):
        d = 2 if k < 2 else WAY[k] % 4
        send(yb.at[d, PART[k]], zbuf.at[k], rz_s.at[k], rz_r.at[k], h_peer[WAY[k]])

    def rz_wait(k):
        landed(zbuf.at[k], rz_s.at[k], rz_r.at[k], h_peer[WAY[k]])

    def rz_mid(k):
        need(rz_wait, k)
        d, part = WAY[k] % 4, PART[k]
        yb[d, part] = (yb[d, part].astype(F32) + zbuf[k].astype(F32)).astype(BF16)
        rz_send(k + 4)

    def rz_end(part):
        t = yb[0, part].astype(F32)
        for k in ENDS[part]:
            need(rz_wait, k)
            t = t + zbuf[k].astype(F32)
        gkv[part * half : (part + 1) * half, :] = t.astype(BF16)

    def gain_part(d, part):
        for k in {0: (), 1: (1, 3), 2: (4, 5), 3: (0, 2)}[d]:
            need(az_wait, k)
        p = mod4(h + d)
        t = yb[d, part].astype(F32) * blk(p, y, c, part)[...].astype(F32)
        fold = t[:, :LANES]
        for i in range(1, kvw // LANES):
            fold = fold + t[:, i * LANES : (i + 1) * LANES]
        gfold[p, pl.ds(pl.multiple_of(c * rows + part * half, half), half), :] = fold

    def gain_send():
        for p in range(4):
            gz[h, p] = jnp.sum(gfold[p].T, axis=0, keepdims=True)
        for s in (1, -1, 2):
            send(gz.at[h], gz.at[h], gg_s.at[8 + s], gg_r.at[8 + s], h_peer[s])

    def gain_pass():
        for s in (1, -1, 2):
            landed(gz.at[mod4(h - s)], gg_s.at[8 + s], gg_r.at[8 + s], h_peer[s])
        mine = y * 2 + c
        for p in range(4):
            gall[mine, p] = gz[0, p] + gz[1, p] + gz[2, p] + gz[3, p]
        for i, peer in enumerate(near):
            send(gall.at[mine], gall.at[mine], gg_s.at[i], gg_r.at[i], peer)

    def gain_end():
        for i, peer in enumerate(near_from):
            landed(gall.at[lax.rem(peer["fsdp"], 8)], gg_s.at[i], gg_r.at[i], near[i])
        for p in range(4):
            for q in range(4):
                lanes = slice((p * 4 + q) * pair, (p * 4 + q + 1) * pair)
                ggain[0:1, lanes] = (gall[2 * q, p] + gall[2 * q + 1, p]) / gain[0:1, lanes]

    def chunk(d, r):
        j = mod4(h + d) * 4 + mod4(y + r)
        lanes = pl.ds(pl.multiple_of(j * pair, pair), pair)
        ng = lax.dot_general(kv[...], wbuf[lanes, :], (((1,), (1,)), ((), ())), preferred_element_type=F32)
        unit = x[:, lanes].astype(F32) * scale[...]
        g = ng * gain[0:1, lanes]
        acc[...] += g * unit
        gb[:, lanes] = g

    def outer_first():
        loads[4].wait()
        width = feat // 4
        for i in range(4):
            dl[i] = delta[:, i * width : (i + 1) * width].astype(BF16)
        for s in (1, 2, 3):
            send(dl.at[mod4(xx + s)], dx.at[s], ox_s.at[s], ox_r.at[s], x_peer[s])

    def outer_second():
        t = dl[xx].astype(F32)
        for s in (1, 2, 3):
            landed(dx.at[s], ox_s.at[s], ox_r.at[s], x_peer[s])
            t = t + dx[s].astype(F32)
        dz[zl] = t.astype(BF16)
        for s in (1, 2, 3):
            send(dz.at[zl], dz.at[zl], og_s.at[0, s], og_r.at[0, s], l_peer[s])

    def outer_third():
        for s in (1, 2, 3):
            landed(dz.at[mod4(zl - s)], og_s.at[0, s], og_r.at[0, s], l_peer[s])
        t = dz[0].astype(F32) + dz[1].astype(F32) + dz[2].astype(F32) + dz[3].astype(F32)
        dt[xx] = t.astype(BF16)
        for s in (1, 2, 3):
            send(dt.at[xx], dt.at[xx], og_s.at[1, s], og_r.at[1, s], x_peer[s])

    def outer_last():
        for s in (1, 2, 3):
            landed(dt.at[mod4(xx - s)], og_s.at[1, s], og_r.at[1, s], x_peer[s])
        loads[5].wait()
        loads[6].wait()
        width = feat // 4
        phase = jnp.full((1, LANES), sync_ref[0].astype(F32)) / ROUNDS
        rate = (OUTER_RATE * (1.0 + jnp.cos(jnp.pi * phase)) / 2.0)[0:1, 0:1]
        for i in range(4):
            at = slice(i * width, (i + 1) * width)
            mean = dt[i].astype(F32) * (1.0 / 16)
            fresh = NESTEROV_MU * mom[:, at] + mean
            nmom[:, at] = fresh
            npar[:, at] = par[:, at] - rate * (mean + NESTEROV_MU * fresh)

    def az_fwd(k):
        need(az_wait, k - 4)
        az_send(k)

    def ay_first(d, part):
        need(az_wait, {(3, 0): 0, (1, 1): 1, (3, 1): 2, (1, 0): 3, (2, 0): 4, (2, 1): 5}[d, part])
        for k in ((0, 3), (1, 2))[part]:
            ay_send(d, k)

    def ay_fwd(d, k):
        need(ay_wait, d, k - 4)
        ay_send(d, k)

    def over(d, r):
        if r == 0:
            for k in {0: (), 1: (1, 3), 2: (4, 5), 3: (0, 2)}[d]:
                need(az_wait, k)
        else:
            for k in {3: (0, 2), 1: (1, 3), 2: (4, 5)}[r]:
                need(ay_wait, d, k)
        as_send(d, r)

    def mul(d, r):
        need(as_wait, d, r)
        chunk(d, r)

    acc[...] = jnp.zeros_like(acc)
    gfold[...] = jnp.zeros_like(gfold)
    kv_here = lambda: landed(kv_sib, nt_s.at[4], nt_r.at[4], sib)
    tasks = dict(
        norm=norm, kv_here=kv_here, partial=partial, az_fwd=az_fwd, ay_first=ay_first, ay_fwd=ay_fwd, over=over,
        mul=mul, ry_mid=ry_mid, ry_end=ry_end, rz_send=rz_send, rz_mid=rz_mid, rz_end=rz_end, gain_part=gain_part,
        gain_send=gain_send, gain_pass=gain_pass, gain_end=gain_end,
        outer_first=outer_first, outer_second=outer_second, outer_third=outer_third, outer_last=outer_last,
    )
    for name, *key in ORDER:
        if outer or not name.startswith("outer"):
            tasks[name](*key)
    inner = jnp.sum(acc[...], axis=-1, keepdims=True) * (1.0 / feat)
    acc[...] = jnp.broadcast_to(inner, acc.shape)

    block = min(64, tok)

    def final(i):
        at = slice(i * block, (i + 1) * block)
        sc, inn = scale[at, :], acc[at, :]
        for j in range(chunks):
            lanes = slice(j * pair, (j + 1) * pair)
            unit = x[at, lanes].astype(F32) * sc
            obuf[at, lanes] = (sc * (gb[at, lanes] - unit * inn)).astype(BF16)

    for i in range(tok // block):
        final(i)
    for name, *key in LATE:
        tasks[name](*key)
    for copy in pending:
        copy.wait_send()


def hand_on(*refs):
    n = len(refs) // 2
    ins, outs, sems = refs[:n], refs[n : 2 * n], refs[2 * n]
    copies = []
    for a, b in zip(ins, outs):
        split = 4 if a.shape[0] >= 256 else 1
        size = a.shape[0] // split
        for i in range(split):
            at = pl.ds(i * size, size)
            copies.append(pltpu.make_async_copy(a.at[at, :], b.at[at, :], sems.at[len(copies)]))
    for copy in copies:
        copy.start()
    for copy in copies:
        copy.wait()


def local(residual_in, norm_gain, kv_weight, kv_grad, outer_delta, outer_momentum, global_params, sync_index, outer=True):
    tok, feat = residual_in.shape[1:]
    rows, kvw = kv_weight.shape[1:]
    frag = outer_delta.shape[1]
    half, pair = rows // 2, 2 * rows
    chunks = feat // pair
    any_space = pl.BlockSpec(memory_space=pl.ANY)
    dma = pltpu.SemaphoreType.DMA
    width = feat // 4
    results = pl.pallas_call(
        functools.partial(kernel, (tok, feat, kvw, outer)),
        out_shape=(
            pltpu.VMEM((rows, kvw), BF16),
            pltpu.VMEM((1, feat), F32),
            pltpu.VMEM((tok, feat), BF16),
            pltpu.VMEM((frag, feat), F32),
            pltpu.VMEM((frag, feat), F32),
        ),
        in_specs=[any_space] * 7 + [pl.BlockSpec(memory_space=pltpu.SMEM)],
        out_specs=(pl.BlockSpec(memory_space=pltpu.VMEM),) * 5,
        scratch_shapes=[
            pltpu.VMEM((tok, feat), BF16),
            pltpu.VMEM((1, feat), F32),
            pltpu.VMEM((feat, kvw), BF16),
            pltpu.VMEM((tok, kvw), BF16),
            pltpu.VMEM((tok, kvw), BF16),
            pltpu.VMEM((2, 4, 4 * rows, tok), BF16),
            pltpu.VMEM((4, 4 * rows, tok), BF16),
            pltpu.VMEM((4, 4 * rows, kvw), BF16),
            pltpu.VMEM((4, 6, half, kvw), BF16),
            pltpu.VMEM((4, 2, half, kvw), BF16),
            pltpu.VMEM((6, half, kvw), BF16),
            pltpu.VMEM((tok, LANES), F32),
            pltpu.VMEM((tok, LANES), F32),
            pltpu.VMEM((tok, feat), F32),
            pltpu.VMEM((4, pair, LANES), F32),
            pltpu.VMEM((4, 4, 1, LANES), F32),
            pltpu.VMEM((8, 4, 1, LANES), F32),
            pltpu.VMEM((frag, feat), F32),
            pltpu.VMEM((frag, feat), F32),
            pltpu.VMEM((frag, feat), F32),
            pltpu.VMEM((4, frag, width), BF16),
            pltpu.VMEM((4, frag, width), BF16),
            pltpu.VMEM((4, frag, width), BF16),
            pltpu.VMEM((4, frag, width), BF16),
            dma((7,)),
            dma((6,)),
            dma((6,)),
            dma((4, 6)),
            dma((4, 6)),
            dma((4, 4)),
            dma((4, 4)),
            dma((5,)),
            dma((5,)),
            dma((4, 6)),
            dma((4, 6)),
            dma((6,)),
            dma((6,)),
            dma((4,)),
            dma((4,)),
            dma((2, 4)),
            dma((2, 4)),
            dma((11,)),
            dma((11,)),
        ],
        compiler_params=pltpu.CompilerParams(
            collective_id=0, has_side_effects=True, vmem_limit_bytes=60 * 1024 * 1024
        ),
    )(
        residual_in[0],
        norm_gain,
        kv_weight[0],
        kv_grad[0],
        outer_delta[0],
        outer_momentum,
        global_params,
        sync_index,
    )
    grad_kv, grad_gain, grad_input, new_params, new_momentum = pl.pallas_call(
        hand_on,
        out_shape=tuple(jax.ShapeDtypeStruct(r.shape, r.dtype) for r in results),
        in_specs=[pl.BlockSpec(memory_space=pltpu.VMEM)] * 5,
        out_specs=(any_space,) * 5,
        scratch_shapes=[dma((8,))],
        compiler_params=pltpu.CompilerParams(vmem_limit_bytes=8 * 1024 * 1024),
    )(*results)
    return (grad_kv[None], grad_gain, grad_input[None], new_params, new_momentum)


def solution(mesh):
    placed = (
        P("rep", "fsdp", None),
        P("rep", None),
        P("rep", "fsdp", None),
        P("rep", "fsdp", None),
        P("rep", "fsdp", None),
        P("fsdp", None),
        P("fsdp", None),
        P(),
    )
    return jax.shard_map(
        local,
        mesh=mesh,
        in_specs=placed,
        out_specs=(
            P("rep", "fsdp", None),
            P("rep", None),
            P("rep", "fsdp", None),
            P("fsdp", None),
            P("fsdp", None),
        ),
        check_vma=False,
    )
```
